32 devices in a mesh: expert: 4 (over z), dp: 8 (over y, x, core).
Axes of the slice: x: 2, y: 2, z: 4, core: 2. Of those that a mesh axis runs over, the one named last changes fastest.
Arguments:
- tokens: bfloat16 [1024, 4096], P(('dp', 'expert')), parts along dimension 0, may hold values from -6 to 6
- expert_ids: int32 [1024, 8], P(('dp', 'expert')), parts along dimension 0, may hold values from 0 to 127, as said below
- gates: bfloat16 [1024, 8], P(('dp', 'expert')), parts along dimension 0, may hold values from 0.099609375 to 1
- weights_in: bfloat16 [4, 4096, 768], P('expert'), may hold values from -0.09375 to 0.09375
- weights_out: bfloat16 [4, 384, 4096], P('expert'), may hold values from -0.21875 to 0.21875
Outputs:
- mixed: bfloat16 [1024, 4096], P(('dp', 'expert')), parts along dimension 0
The draws below stay inside these ranges and needn't reach their ends.
There are 8 independent parts, one for each index of `dp`. The reference program is written for one: setup_inputs(seed, part) draws one part's arguments, and reference() takes and returns one part's arrays. A program takes and returns all parts, laid end to end along the dimension named above; an argument that names none is the same for every part. Nothing has to cross between parts.
Inputs may be any that keep to these rules, and one draw needn't show every extreme that they name: `expert_ids`: each row names 8 different experts. Of one device's 32 rows, each expert of 0 to 1 is named by at most 8 rows; one such expert is named by exactly 8 rows of every device, the others by at most 4 rows of each device and at least one.
All inputs are finite; a program needn't handle non-finite values.
Results may differ from the reference program's by a relative error of at most 0.0095.
Values may be sent and summed in bfloat16 or wider, within the bound.
A program may use at most 64 MiB of HBM per device.

```python
import jax
import jax.numpy as jnp
from jax import lax

D = 4096
EXPERTS = 128
TOP = 8
TOK_DEV = 32
FFW = 768
HID = 384
FLIGHT = 2
SLICES = 4
TOKENS = 128
SRC_CAP = 8
N_EXPERT = 4


def draw_expert_ids(key, part):
    keys = jax.random.split(jax.random.fold_in(key, 11), 4)
    blocks = TOKENS // TOK_DEV
    hottest = jax.random.randint(keys[0], (), 0, FLIGHT)
    lowest = (SRC_CAP + 3) // 4
    highest = SRC_CAP // 2 + 1
    counts = jax.random.randint(keys[1], (FLIGHT, blocks), lowest, highest)
    counts = jnp.where(jnp.arange(FLIGHT)[:, None] == hottest, SRC_CAP, counts)
    scores = jax.random.randint(keys[2], (FLIGHT, blocks, TOK_DEV), 0, 2 ** 20) * TOK_DEV + jnp.arange(TOK_DEV)[None, None, :]
    ranks = jnp.argsort(jnp.argsort(scores, axis=2, stable=True), axis=2, stable=True)
    member = (ranks < counts[:, :, None]).reshape(FLIGHT, TOKENS).T
    others = jax.random.randint(keys[3], (TOKENS, EXPERTS), 0, 2 ** 20) * EXPERTS + jnp.arange(EXPERTS)[None, :]
    flight_part = jnp.where(member, others[:, :FLIGHT] + 2 ** 28, -1)
    combined = jnp.concatenate([flight_part, others[:, FLIGHT:]], axis=1)
    chosen = lax.top_k(combined, TOP)[1]
    return chosen.astype(jnp.int32)


def level_of(stream_key, extent, cuts, least, largest):
    factor_of, own = 1.0, jax.random.fold_in(stream_key, 6)
    for dim, parts in cuts:
        draws = jnp.exp(jax.random.uniform(jax.random.fold_in(own, dim), (parts,), jnp.float32, least / len(cuts), largest / len(cuts)))
        factor_of = factor_of * jnp.repeat(draws, extent[dim] // parts).reshape([-1 if axis == dim else 1 for axis in range(len(extent))])
    return factor_of


def normal_values(key, dims, scale, bound, shards=(), held_as=jnp.bfloat16):
    entries = scale * jax.random.normal(key, dims, jnp.float32)
    if shards:
        entries = entries * level_of(key, dims, shards, -0.22, 0.18)
    return jnp.clip(entries, -bound, bound).astype(held_as)


def setup_inputs(seed: int = 0, part: int = 0) -> dict:
    arg_keys = jax.random.split(jax.random.key(seed), 6)
    part_splits = jax.random.split(jax.random.fold_in(arg_keys[5], part), 6)
    return {
        "tokens": normal_values(part_splits[0], (TOKENS, D), 1.0, 6.0, ((0, 4),)),
        "expert_ids": draw_expert_ids(jax.random.fold_in(jax.random.fold_in(arg_keys[5], part), 71), part),
        "gates": jnp.clip(0.099609375 + 0.9003906 * jax.random.uniform(part_splits[2], (TOKENS, TOP), jnp.float32) ** level_of(part_splits[2], (TOKENS, TOP), ((0, 4),), -0.2, 0.2), 0.099609375, 1.0).astype(jnp.bfloat16),
        "weights_in": normal_values(arg_keys[3], (SLICES, D, 2 * HID), D ** -0.5, 0.09375, ((0, 4),)),
        "weights_out": normal_values(arg_keys[4], (SLICES, HID, D), FFW ** -0.5, 0.21875, ((0, 4),)),
    }


def route_weights(expert_ids, gates, flight):
    expert_range = jnp.arange(flight, dtype=jnp.int32)
    matches = expert_ids[:, :, None] == expert_range[None, None, :]
    return jnp.sum(jnp.where(matches, gates[:, :, None], jnp.zeros((), gates.dtype)), axis=1)


def pick_slots(routed, capacity):
    position = jnp.cumsum(routed.astype(jnp.int32)) - 1
    slot_ids = jnp.arange(capacity, dtype=jnp.int32)
    matches = (position[None, :] == slot_ids[:, None]) & routed[None, :]
    row_ids = jnp.arange(routed.shape[0], dtype=jnp.int32)
    token_index = jnp.sum(matches.astype(jnp.int32) * row_ids[None, :], axis=1).astype(jnp.int32)
    filled = jnp.any(matches, axis=1)
    return token_index, filled


def expert_rows(picked, slot_gate, weights_in, weights_out):
    hidden_units = weights_out.shape[0]
    merged = jnp.dot(picked, weights_in, preferred_element_type=jnp.float32)
    hidden = (jax.nn.silu(merged[:, :hidden_units]) * merged[:, hidden_units:]).astype(jnp.bfloat16)
    output = jnp.dot(hidden, weights_out, preferred_element_type=jnp.float32)
    return output * slot_gate.astype(jnp.float32)[:, None]


def reference(tokens, expert_ids, gates, weights_in, weights_out):
    weight_table = route_weights(expert_ids, gates, FLIGHT).astype(jnp.float32)
    capacity = SRC_CAP * N_EXPERT
    expert_range = jnp.arange(FLIGHT, dtype=jnp.int32)

    def step(total, inputs):
        slice_in, slice_out, slice_index = inputs
        column = jnp.sum(jnp.where(expert_range[None, :] == slice_index // 2, weight_table, jnp.zeros((), jnp.float32)), axis=1)
        token_index, filled = pick_slots(column > 0, capacity)
        picked = tokens[token_index]
        slot_gate = jnp.where(filled, column[token_index], jnp.zeros((), jnp.float32))
        output = expert_rows(picked, slot_gate, slice_in, slice_out)
        rounded = lax.optimization_barrier(output.astype(jnp.bfloat16)).astype(jnp.float32)
        return total.at[token_index].add(rounded), None

    initial = jnp.zeros((TOKENS, D), jnp.float32)
    total, _ = lax.scan(step, initial, (weights_in, weights_out, jnp.arange(SLICES, dtype=jnp.int32)))
    return total.astype(jnp.bfloat16)
```

```python
from functools import partial

import jax
import jax.numpy as jnp
from jax import lax
from jax.experimental import pallas as pl
from jax.experimental.pallas import tpu as pltpu
from jax.sharding import PartitionSpec as P

SRC_CAP = 8
PACK = 2 * SRC_CAP
IN_CHUNKS = 4
OUT_CHUNKS = 4
MESH = pl.DeviceIdType.MESH


def slot_matrix(value, routed, position, rows, rows_per_expert):
    tokens = value[0].shape[1]
    row = lax.broadcasted_iota(jnp.int32, (rows, tokens), 0)
    slot = (row % SRC_CAP).astype(jnp.float32)
    expert = row // rows_per_expert
    table = jnp.zeros((rows, tokens), jnp.float32)
    for e in range(len(value)):
        hit = (expert == e) & (position[e] == slot) & (routed[e] > 0.0)
        table = jnp.where(hit, value[e], table)
    return table


def split_halves(table, axis):
    half = (lax.broadcasted_iota(jnp.int32, table.shape, axis) // SRC_CAP) % 2
    zero = jnp.zeros_like(table)
    return jnp.where(half == 0, table, zero), jnp.where(half == 1, table, zero)


def kernel(
    n,
    tok_hbm,
    ids_hbm,
    gate_hbm,
    win_hbm,
    wout_hbm,
    out_ref,
    tok,
    ids,
    gate,
    win,
    wout,
    send_rows,
    recv_rows,
    send_out,
    recv_out,
    small_sem,
    win_sem,
    wout_sem,
    row_send_sem,
    row_recv_sem,
    out_send_sem,
    out_recv_sem,
):
    me = lax.axis_index("expert")
    flight = n // 2
    width = tok.shape[1]
    hid = wout.shape[0]
    in_width = width // IN_CHUNKS
    in_half = in_width // 2
    out_width = width // OUT_CHUNKS
    out_half = out_width // 2

    def peer(d):
        return lax.rem(me + d, n)

    barrier = pltpu.get_barrier_semaphore()
    for d in range(1, n):
        pl.semaphore_signal(barrier, inc=1, device_id={"expert": peer(d)}, device_id_type=MESH)

    small = [
        pltpu.make_async_copy(ids_hbm, ids, small_sem.at[0]),
        pltpu.make_async_copy(gate_hbm, gate, small_sem.at[1]),
        pltpu.make_async_copy(tok_hbm, tok, small_sem.at[2]),
    ]
    for copy in small:
        copy.start()

    def win_copy(c):
        rows = pl.ds(c * in_width, in_width)
        return pltpu.make_async_copy(win_hbm.at[0, rows], win.at[rows], win_sem.at[c])

    wout_copy = pltpu.make_async_copy(wout_hbm.at[0], wout, wout_sem)
    for c in range(IN_CHUNKS):
        win_copy(c).start()
    wout_copy.start()

    small[0].wait()
    small[1].wait()
    chosen = ids[...]
    gates = gate[...].astype(jnp.float32)
    tokens = chosen.shape[1]
    weight, routed = [], []
    for e in range(flight):
        match = chosen == e
        weight.append(jnp.sum(jnp.where(match, gates, 0.0), axis=0, keepdims=True))
        routed.append(jnp.sum(jnp.where(match, 1.0, 0.0), axis=0, keepdims=True))
    row = lax.broadcasted_iota(jnp.int32, (PACK, tokens), 0)
    marks = jnp.zeros((PACK, tokens), jnp.float32)
    for e in range(flight):
        marks = jnp.where(row == e, routed[e], marks)
    before = lax.broadcasted_iota(jnp.int32, (tokens, tokens), 0) < lax.broadcasted_iota(
        jnp.int32, (tokens, tokens), 1
    )
    ahead = jnp.dot(
        marks.astype(jnp.bfloat16),
        before.astype(jnp.float32).astype(jnp.bfloat16),
        preferred_element_type=jnp.float32,
    )
    position = [ahead[e : e + 1] for e in range(flight)]
    pick = slot_matrix(routed, routed, position, flight * PACK, PACK)
    pick = [part.astype(jnp.bfloat16) for part in split_halves(pick, 0)]

    def row_copy(d, c):
        dst = peer(d)
        return pltpu.make_async_remote_copy(
            src_ref=send_rows.at[dst // 2, c],
            dst_ref=recv_rows.at[me, c],
            send_sem=row_send_sem.at[dst, c],
            recv_sem=row_recv_sem.at[me, c],
            device_id={"expert": dst},
            device_id_type=MESH,
        )

    def row_arrival(d, c):
        src = peer(d)
        return pltpu.make_async_remote_copy(
            src_ref=send_rows.at[0, c],
            dst_ref=recv_rows.at[src, c],
            send_sem=row_send_sem.at[src, c],
            recv_sem=row_recv_sem.at[src, c],
            device_id={"expert": src},
            device_id_type=MESH,
        )

    small[2].wait()
    for c in range(IN_CHUNKS):
        lo = c * in_width
        rows = sum(
            jnp.dot(
                pick[half],
                tok[:, lo + half * in_half : lo + (half + 1) * in_half],
                preferred_element_type=jnp.float32,
            )
            for half in range(2)
        ).astype(jnp.bfloat16)
        send_rows[:, c] = rows.reshape(flight, PACK, in_half)
        if c == 0:
            pl.semaphore_wait(barrier, n - 1)
        for d in range(1, n):
            row_copy(d, c).start()
        recv_rows[me, c] = send_rows[me // 2, c]

    combine = jnp.transpose(slot_matrix(weight, routed, position, n * PACK, 2 * PACK))
    combine = jnp.concatenate(split_halves(combine, 1), axis=0).astype(jnp.bfloat16)

    def in_step(c, total):
        win_copy(c).wait()
        for d in range(1, n):
            row_arrival(d, c).wait_recv()
        packed = recv_rows[:, c].astype(jnp.float32)
        for half in range(2):
            rows = packed[:, half * SRC_CAP : (half + 1) * SRC_CAP].reshape(n * SRC_CAP, in_half)
            start = pl.multiple_of(c * in_width + half * in_half, in_half)
            total = total + jnp.dot(
                rows.astype(jnp.bfloat16),
                win[pl.ds(start, in_half)],
                preferred_element_type=jnp.float32,
            )
        return total

    merged = lax.fori_loop(
        0, IN_CHUNKS, in_step, jnp.zeros((n * SRC_CAP, 2 * hid), jnp.float32)
    )
    left = merged[:, :hid]
    hidden = (left / (1.0 + jnp.exp(-left)) * merged[:, hid:]).astype(jnp.bfloat16)

    def out_copy(d, c):
        dst = peer(d)
        return pltpu.make_async_remote_copy(
            src_ref=send_out.at[dst, c],
            dst_ref=recv_out.at[me, c],
            send_sem=out_send_sem.at[dst, c],
            recv_sem=out_recv_sem.at[me, c],
            device_id={"expert": dst},
            device_id_type=MESH,
        )

    def out_arrival(d, c):
        src = peer(d)
        return pltpu.make_async_remote_copy(
            src_ref=send_out.at[src, c],
            dst_ref=recv_out.at[src, c],
            send_sem=out_send_sem.at[src, c],
            recv_sem=out_recv_sem.at[src, c],
            device_id={"expert": src},
            device_id_type=MESH,
        )

    wout_copy.wait()
    for c in range(OUT_CHUNKS):
        lo = c * out_width
        output = jnp.dot(
            hidden, wout[:, lo : lo + out_width], preferred_element_type=jnp.float32
        ).reshape(n, SRC_CAP, out_width)
        packed = jnp.concatenate([output[:, :, :out_half], output[:, :, out_half:]], axis=1)
        send_out[:, c] = packed.astype(jnp.bfloat16)
        for d in range(1, n):
            out_copy(d, c).start()
        recv_out[me, c] = send_out[me, c]

    for c in range(OUT_CHUNKS):
        lo = c * out_width
        for d in range(1, n):
            out_arrival(d, c).wait_recv()
        packed = recv_out[:, c].reshape(n * PACK, out_half)
        mixed = jnp.dot(combine, packed, preferred_element_type=jnp.float32).astype(jnp.bfloat16)
        out_ref[:, lo : lo + out_half] = mixed[:tokens]
        out_ref[:, lo + out_half : lo + out_width] = mixed[tokens:]

    for c in range(IN_CHUNKS):
        for d in range(1, n):
            row_copy(d, c).wait_send()
    for c in range(OUT_CHUNKS):
        for d in range(1, n):
            out_copy(d, c).wait_send()


def body(tokens, expert_ids, gates, weights_in, weights_out):
    n = lax.axis_size("expert")
    flight = n // 2
    local, width = tokens.shape
    hid = weights_out.shape[1]
    in_half = width // IN_CHUNKS // 2
    out_half = width // OUT_CHUNKS // 2
    dtype = tokens.dtype
    return pl.pallas_call(
        partial(kernel, n),
        out_shape=jax.ShapeDtypeStruct((local, width), dtype),
        in_specs=[pl.BlockSpec(memory_space=pl.ANY)] * 5,
        out_specs=pl.BlockSpec(memory_space=pltpu.VMEM),
        scratch_shapes=[
            pltpu.VMEM((local, width), dtype),
            pltpu.VMEM(expert_ids.shape[::-1], expert_ids.dtype),
            pltpu.VMEM(gates.shape[::-1], gates.dtype),
            pltpu.VMEM(weights_in.shape[1:], weights_in.dtype),
            pltpu.VMEM(weights_out.shape[1:], weights_out.dtype),
            pltpu.VMEM((flight, IN_CHUNKS, PACK, in_half), dtype),
            pltpu.VMEM((n, IN_CHUNKS, PACK, in_half), dtype),
            pltpu.VMEM((n, OUT_CHUNKS, PACK, out_half), dtype),
            pltpu.VMEM((n, OUT_CHUNKS, PACK, out_half), dtype),
            pltpu.SemaphoreType.DMA((3,)),
            pltpu.SemaphoreType.DMA((IN_CHUNKS,)),
            pltpu.SemaphoreType.DMA,
            pltpu.SemaphoreType.DMA((n, IN_CHUNKS)),
            pltpu.SemaphoreType.DMA((n, IN_CHUNKS)),
            pltpu.SemaphoreType.DMA((n, OUT_CHUNKS)),
            pltpu.SemaphoreType.DMA((n, OUT_CHUNKS)),
        ],
        compiler_params=pltpu.CompilerParams(
            collective_id=0, has_side_effects=True, vmem_limit_bytes=62 * 2**20
        ),
    )(tokens, expert_ids.T, gates.T, weights_in, weights_out)


def solution(mesh):
    return jax.shard_map(
        body,
        mesh=mesh,
        in_specs=(
            P(("dp", "expert"), None),
            P(("dp", "expert"), None),
            P(("dp", "expert"), None),
            P("expert", None, None),
            P("expert", None, None),
        ),
        out_specs=P(("dp", "expert"), None),
        check_vma=False,
    )
```

```python
from functools import partial

import jax
import jax.numpy as jnp
from jax import lax
from jax.experimental import pallas as pl
from jax.experimental.pallas import tpu as pltpu
from jax.sharding import PartitionSpec as P

SRC_CAP = 8
PACK = 2 * SRC_CAP
IN_CHUNKS = 4
OUT_CHUNKS = 4
MESH = pl.DeviceIdType.MESH


def slot_matrix(value, routed, position, rows, rows_per_expert):
    tokens = value[0].shape[1]
    row = lax.broadcasted_iota(jnp.int32, (rows, tokens), 0)
    slot = (row % SRC_CAP).astype(jnp.float32)
    expert = row // rows_per_expert
    table = jnp.zeros((rows, tokens), jnp.float32)
    for e in range(len(value)):
        hit = (expert == e) & (position[e] == slot) & (routed[e] > 0.0)
        table = jnp.where(hit, value[e], table)
    return table


def split_halves(table, axis):
    half = (lax.broadcasted_iota(jnp.int32, table.shape, axis) // SRC_CAP) % 2
    zero = jnp.zeros_like(table)
    return jnp.where(half == 0, table, zero), jnp.where(half == 1, table, zero)


def kernel(
    n,
    tok_hbm,
    ids_hbm,
    gate_hbm,
    win_hbm,
    wout_hbm,
    out_ref,
    tok,
    ids,
    gate,
    win,
    wout,
    send_rows,
    recv_rows,
    send_out,
    recv_out,
    small_sem,
    win_sem,
    wout_sem,
    row_send_sem,
    row_recv_sem,
    out_send_sem,
    out_recv_sem,
):
    me = lax.axis_index("expert")
    flight = n // 2
    width = tok.shape[1]
    hid = wout.shape[0]
    in_width = width // IN_CHUNKS
    in_half = in_width // 2
    out_width = width // OUT_CHUNKS
    out_half = out_width // 2

    def peer(d):
        return lax.rem(me + d, n)

    barrier = pltpu.get_barrier_semaphore()
    for d in range(1, n):
        pl.semaphore_signal(barrier, inc=1, device_id={"expert": peer(d)}, device_id_type=MESH)

    small = [
        pltpu.make_async_copy(ids_hbm, ids, small_sem.at[0]),
        pltpu.make_async_copy(gate_hbm, gate, small_sem.at[1]),
        pltpu.make_async_copy(tok_hbm, tok, small_sem.at[2]),
    ]
    for copy in small:
        copy.start()

    def win_copy(c):
        rows = pl.ds(c * in_width, in_width)
        return pltpu.make_async_copy(win_hbm.at[0, rows], win.at[rows], win_sem.at[c])

    wout_copy = pltpu.make_async_copy(wout_hbm.at[0], wout, wout_sem)
    for c in range(IN_CHUNKS):
        win_copy(c).start()
    wout_copy.start()

    small[0].wait()
    small[1].wait()
    chosen = ids[...]
    gates = gate[...].astype(jnp.float32)
    tokens = chosen.shape[1]
    weight, routed = [], []
    for e in range(flight):
        match = chosen == e
        weight.append(jnp.sum(jnp.where(match, gates, 0.0), axis=0, keepdims=True))
        routed.append(jnp.sum(jnp.where(match, 1.0, 0.0), axis=0, keepdims=True))
    row = lax.broadcasted_iota(jnp.int32, (PACK, tokens), 0)
    marks = jnp.zeros((PACK, tokens), jnp.float32)
    for e in range(flight):
        marks = jnp.where(row == e, routed[e], marks)
    before = lax.broadcasted_iota(jnp.int32, (tokens, tokens), 0) < lax.broadcasted_iota(
        jnp.int32, (tokens, tokens), 1
    )
    ahead = jnp.dot(
        marks.astype(jnp.bfloat16),
        before.astype(jnp.float32).astype(jnp.bfloat16),
        preferred_element_type=jnp.float32,
    )
    position = [ahead[e : e + 1] for e in range(flight)]
    pick = slot_matrix(routed, routed, position, flight * PACK, PACK)
    pick = [part.astype(jnp.bfloat16) for part in split_halves(pick, 0)]

    def row_copy(d, c):
        dst = peer(d)
        return pltpu.make_async_remote_copy(
            src_ref=send_rows.at[dst // 2, c],
            dst_ref=recv_rows.at[me, c],
            send_sem=row_send_sem.at[dst, c],
            recv_sem=row_recv_sem.at[me, c],
            device_id={"expert": dst},
            device_id_type=MESH,
        )

    def row_arrival(d, c):
        src = peer(d)
        return pltpu.make_async_remote_copy(
            src_ref=send_rows.at[0, c],
            dst_ref=recv_rows.at[src, c],
            send_sem=row_send_sem.at[src, c],
            recv_sem=row_recv_sem.at[src, c],
            device_id={"expert": src},
            device_id_type=MESH,
        )

    small[2].wait()
    for c in range(IN_CHUNKS):
        lo = c * in_width
        rows = sum(
            jnp.dot(
                pick[half],
                tok[:, lo + half * in_half : lo + (half + 1) * in_half],
                preferred_element_type=jnp.float32,
            )
            for half in range(2)
        ).astype(jnp.bfloat16)
        send_rows[:, c] = rows.reshape(flight, PACK, in_half)
        if c == 0:
            pl.semaphore_wait(barrier, n - 1)
        for d in range(1, n):
            row_copy(d, c).start()
        recv_rows[me, c] = send_rows[me // 2, c]

    combine = jnp.transpose(slot_matrix(weight, routed, position, n * PACK, 2 * PACK))
    combine = jnp.concatenate(split_halves(combine, 1), axis=0).astype(jnp.bfloat16)

    def in_step(c, total):
        win_copy(c).wait()
        for d in range(1, n):
            row_arrival(d, c).wait_recv()
        packed = recv_rows[:, c].astype(jnp.float32)
        for half in range(2):
            rows = packed[:, half * SRC_CAP : (half + 1) * SRC_CAP].reshape(n * SRC_CAP, in_half)
            start = pl.multiple_of(c * in_width + half * in_half, in_half)
            total = total + jnp.dot(
                rows.astype(jnp.bfloat16),
                win[pl.ds(start, in_half)],
                preferred_element_type=jnp.float32,
            )
        return total

    merged = lax.fori_loop(
        0, IN_CHUNKS, in_step, jnp.zeros((n * SRC_CAP, 2 * hid), jnp.float32)
    )
    left = merged[:, :hid]
    hidden = (left / (1.0 + jnp.exp(-left)) * merged[:, hid:]).astype(jnp.bfloat16)

    def out_copy(d, c):
        dst = peer(d)
        return pltpu.make_async_remote_copy(
            src_ref=send_out.at[dst, c],
            dst_ref=recv_out.at[me, c],
            send_sem=out_send_sem.at[dst, c],
            recv_sem=out_recv_sem.at[me, c],
            device_id={"expert": dst},
            device_id_type=MESH,
        )

    def out_arrival(d, c):
        src = peer(d)
        return pltpu.make_async_remote_copy(
            src_ref=send_out.at[src, c],
            dst_ref=recv_out.at[src, c],
            send_sem=out_send_sem.at[src, c],
            recv_sem=out_recv_sem.at[src, c],
            device_id={"expert": src},
            device_id_type=MESH,
        )

    wout_copy.wait()
    for c in range(OUT_CHUNKS):
        lo = c * out_width
        output = jnp.dot(
            hidden, wout[:, lo : lo + out_width], preferred_element_type=jnp.float32
        ).reshape(n, SRC_CAP, out_width)
        packed = jnp.concatenate([output[:, :, :out_half], output[:, :, out_half:]], axis=1)
        send_out[:, c] = packed.astype(jnp.bfloat16)
        for d in range(1, n):
            out_copy(d, c).start()
        recv_out[me, c] = send_out[me, c]

    for c in range(OUT_CHUNKS):
        lo = c * out_width
        for d in range(1, n):
            out_arrival(d, c).wait_recv()
        packed = recv_out[:, c].reshape(n * PACK, out_half)
        mixed = jnp.dot(combine, packed, preferred_element_type=jnp.float32).astype(jnp.bfloat16)
        out_ref[:, lo : lo + out_half] = mixed[:tokens]
        out_ref[:, lo + out_half : lo + out_width] = mixed[tokens:]

    for c in range(IN_CHUNKS):
        for d in range(1, n):
            row_copy(d, c).wait_send()
    for c in range(OUT_CHUNKS):
        for d in range(1, n):
            out_copy(d, c).wait_send()


def body(tokens, expert_ids, gates, weights_in, weights_out):
    n = lax.axis_size("expert")
    flight = n // 2
    local, width = tokens.shape
    hid = weights_out.shape[1]
    in_half = width // IN_CHUNKS // 2
    out_half = width // OUT_CHUNKS // 2
    dtype = tokens.dtype
    return pl.pallas_call(
        partial(kernel, n),
        out_shape=pltpu.VMEM((local, width), dtype),
        in_specs=[pl.BlockSpec(memory_space=pltpu.HBM)] * 5,
        out_specs=pl.BlockSpec(memory_space=pltpu.VMEM),
        scratch_shapes=[
            pltpu.VMEM((local, width), dtype),
            pltpu.VMEM(expert_ids.shape[::-1], expert_ids.dtype),
            pltpu.VMEM(gates.shape[::-1], gates.dtype),
            pltpu.VMEM(weights_in.shape[1:], weights_in.dtype),
            pltpu.VMEM(weights_out.shape[1:], weights_out.dtype),
            pltpu.VMEM((flight, IN_CHUNKS, PACK, in_half), dtype),
            pltpu.VMEM((n, IN_CHUNKS, PACK, in_half), dtype),
            pltpu.VMEM((n, OUT_CHUNKS, PACK, out_half), dtype),
            pltpu.VMEM((n, OUT_CHUNKS, PACK, out_half), dtype),
            pltpu.SemaphoreType.DMA((3,)),
            pltpu.SemaphoreType.DMA((IN_CHUNKS,)),
            pltpu.SemaphoreType.DMA,
            pltpu.SemaphoreType.DMA((n, IN_CHUNKS)),
            pltpu.SemaphoreType.DMA((n, IN_CHUNKS)),
            pltpu.SemaphoreType.DMA((n, OUT_CHUNKS)),
            pltpu.SemaphoreType.DMA((n, OUT_CHUNKS)),
        ],
        compiler_params=pltpu.CompilerParams(
            collective_id=0, has_side_effects=True, vmem_limit_bytes=56 * 2**20
        ),
    )(tokens, expert_ids.T, gates.T, weights_in, weights_out)


def solution(mesh):
    return jax.shard_map(
        body,
        mesh=mesh,
        in_specs=(
            P(("dp", "expert"), None),
            P(("dp", "expert"), None),
            P(("dp", "expert"), None),
            P("expert", None, None),
            P("expert", None, None),
        ),
        out_specs=P(("dp", "expert"), None),
        check_vma=False,
    )
```

```python
from functools import partial

import jax
import jax.numpy as jnp
from jax import lax
from jax.experimental import pallas as pl
from jax.experimental.pallas import tpu as pltpu
from jax.sharding import PartitionSpec as P

SRC_CAP = 8
PACK = 2 * SRC_CAP
IN_CHUNKS = 4
OUT_CHUNKS = 4
RELAY_IN = 2
RELAY_OUT = 2
MESH = pl.DeviceIdType.MESH


def slot_matrix(value, routed, position, rows, rows_per_expert):
    tokens = value[0].shape[1]
    row = lax.broadcasted_iota(jnp.int32, (rows, tokens), 0)
    slot = (row % SRC_CAP).astype(jnp.float32)
    expert = row // rows_per_expert
    table = jnp.zeros((rows, tokens), jnp.float32)
    for e in range(len(value)):
        hit = (expert == e) & (position[e] == slot) & (routed[e] > 0.0)
        table = jnp.where(hit, value[e], table)
    return table


def split_halves(table, axis):
    half = (lax.broadcasted_iota(jnp.int32, table.shape, axis) // SRC_CAP) % 2
    zero = jnp.zeros_like(table)
    return jnp.where(half == 0, table, zero), jnp.where(half == 1, table, zero)


def kernel(
    n,
    tok_hbm,
    ids_hbm,
    gate_hbm,
    win_hbm,
    wout_hbm,
    out_ref,
    tok,
    ids,
    gate,
    win,
    wout,
    send_rows,
    recv_rows,
    send_out,
    recv_out,
    partial_out,
    small_sem,
    win_sem,
    wout_sem,
    row_send_sem,
    row_recv_sem,
    out_send_sem,
    out_recv_sem,
    relay_sem,
    partial_sem,
):
    me = lax.axis_index("expert")
    flight = n // 2
    width = tok.shape[1]
    hid = wout.shape[0]
    in_width = width // IN_CHUNKS
    in_half = in_width // 2
    out_width = width // OUT_CHUNKS
    out_half = out_width // 2

    pair = me // 2
    partner = me + 1 - 2 * (me % 2)

    def peer(d):
        return lax.rem(me + d, n)

    def other_pair(k):
        return lax.rem(pair + k, flight)

    def near_of(source, target_pair):
        return 2 * target_pair + jnp.where(source < 2 * target_pair, 0, 1)

    def others():
        for k in range(1, flight):
            for member in range(2):
                yield 2 * other_pair(k) + member

    barrier = pltpu.get_barrier_semaphore()
    for d in range(1, n):
        pl.semaphore_signal(barrier, inc=1, device_id={"expert": peer(d)}, device_id_type=MESH)

    small = [
        pltpu.make_async_copy(ids_hbm, ids, small_sem.at[0]),
        pltpu.make_async_copy(gate_hbm, gate, small_sem.at[1]),
        pltpu.make_async_copy(tok_hbm, tok, small_sem.at[2]),
    ]
    for copy in small:
        copy.start()

    def win_copy(c):
        rows = pl.ds(c * in_width, in_width)
        return pltpu.make_async_copy(win_hbm.at[0, rows], win.at[rows], win_sem.at[c])

    wout_copy = pltpu.make_async_copy(wout_hbm.at[0], wout, wout_sem)
    for c in range(IN_CHUNKS):
        win_copy(c).start()
    wout_copy.start()

    small[0].wait()
    small[1].wait()
    chosen = ids[...]
    gates = gate[...].astype(jnp.float32)
    tokens = chosen.shape[1]
    weight, routed = [], []
    for e in range(flight):
        match = chosen == e
        weight.append(jnp.sum(jnp.where(match, gates, 0.0), axis=0, keepdims=True))
        routed.append(jnp.sum(jnp.where(match, 1.0, 0.0), axis=0, keepdims=True))
    row = lax.broadcasted_iota(jnp.int32, (PACK, tokens), 0)
    marks = jnp.zeros((PACK, tokens), jnp.float32)
    for e in range(flight):
        marks = jnp.where(row == e, routed[e], marks)
    before = lax.broadcasted_iota(jnp.int32, (tokens, tokens), 0) < lax.broadcasted_iota(
        jnp.int32, (tokens, tokens), 1
    )
    ahead = jnp.dot(
        marks.astype(jnp.bfloat16),
        before.astype(jnp.float32).astype(jnp.bfloat16),
        preferred_element_type=jnp.float32,
    )
    position = [ahead[e : e + 1] for e in range(flight)]
    pick = slot_matrix(routed, routed, position, flight * PACK, PACK)
    pick = [part.astype(jnp.bfloat16) for part in split_halves(pick, 0)]

    def row_copy(dst, c):
        return pltpu.make_async_remote_copy(
            src_ref=send_rows.at[dst // 2, c],
            dst_ref=recv_rows.at[me, c],
            send_sem=row_send_sem.at[dst, c],
            recv_sem=row_recv_sem.at[me, c],
            device_id={"expert": dst},
            device_id_type=MESH,
        )

    def relay_copy(src, c):
        return pltpu.make_async_remote_copy(
            src_ref=recv_rows.at[src, c],
            dst_ref=recv_rows.at[src, c],
            send_sem=relay_sem.at[src, c],
            recv_sem=row_recv_sem.at[src, c],
            device_id={"expert": partner},
            device_id_type=MESH,
        )

    def row_targets(c):
        for k in range(1, flight):
            near = near_of(me, other_pair(k))
            yield near
            if c >= RELAY_IN:
                yield 4 * other_pair(k) + 1 - near
        yield partner

    small[2].wait()
    for c in range(IN_CHUNKS):
        lo = c * in_width
        rows = sum(
            jnp.dot(
                pick[half],
                tok[:, lo + half * in_half : lo + (half + 1) * in_half],
                preferred_element_type=jnp.float32,
            )
            for half in range(2)
        ).astype(jnp.bfloat16)
        send_rows[:, c] = rows.reshape(flight, PACK, in_half)
        if c == 0:
            pl.semaphore_wait(barrier, n - 1)
        for dst in row_targets(c):
            row_copy(dst, c).start()
        recv_rows[me, c] = send_rows[me // 2, c]

    combine = jnp.transpose(slot_matrix(weight, routed, position, n * PACK, 2 * PACK))
    combine = jnp.concatenate(split_halves(combine, 1), axis=0).astype(jnp.bfloat16)

    def in_step(c, total):
        win_copy(c).wait()
        for src in others():
            relay_copy(src, c).wait_recv()

            @pl.when((near_of(src, pair) == me) & (c < RELAY_IN))
            def _():
                relay_copy(src, c).start()

        relay_copy(partner, c).wait_recv()
        packed = recv_rows[:, c].astype(jnp.float32)
        for half in range(2):
            rows = packed[:, half * SRC_CAP : (half + 1) * SRC_CAP].reshape(n * SRC_CAP, in_half)
            start = pl.multiple_of(c * in_width + half * in_half, in_half)
            total = total + jnp.dot(
                rows.astype(jnp.bfloat16),
                win[pl.ds(start, in_half)],
                preferred_element_type=jnp.float32,
            )
        return total

    merged = lax.fori_loop(
        0, IN_CHUNKS, in_step, jnp.zeros((n * SRC_CAP, 2 * hid), jnp.float32)
    )
    left = merged[:, :hid]
    hidden = (left / (1.0 + jnp.exp(-left)) * merged[:, hid:]).astype(jnp.bfloat16)

    def out_copy(dst, c, slot):
        return pltpu.make_async_remote_copy(
            src_ref=send_out.at[dst, c],
            dst_ref=recv_out.at[slot, c],
            send_sem=out_send_sem.at[dst, c],
            recv_sem=out_recv_sem.at[slot, c],
            device_id={"expert": dst},
            device_id_type=MESH,
        )

    def partial_copy(dst, c):
        return pltpu.make_async_remote_copy(
            src_ref=send_out.at[dst, c],
            dst_ref=partial_out.at[dst, c],
            send_sem=out_send_sem.at[dst, c],
            recv_sem=partial_sem.at[dst, c],
            device_id={"expert": partner},
            device_id_type=MESH,
        )

    wout_copy.wait()
    for c in range(OUT_CHUNKS):
        lo = c * out_width
        output = jnp.dot(
            hidden, wout[:, lo : lo + out_width], preferred_element_type=jnp.float32
        ).reshape(n, SRC_CAP, out_width)
        packed = jnp.concatenate([output[:, :, :out_half], output[:, :, out_half:]], axis=1)
        send_out[:, c] = packed.astype(jnp.bfloat16)
        for dst in others():
            if c < RELAY_OUT:

                @pl.when(near_of(dst, pair) != me)
                def _():
                    partial_copy(dst, c).start()
            else:
                out_copy(dst, c, me).start()
        out_copy(partner, c, me).start()
        recv_out[me, c] = send_out[me, c]

    for c in range(RELAY_OUT):
        for dst in others():

            @pl.when(near_of(dst, pair) == me)
            def _():
                partial_copy(dst, c).wait_recv()
                both = send_out[dst, c].astype(jnp.float32) + partial_out[dst, c].astype(
                    jnp.float32
                )
                send_out[dst, c] = both.astype(jnp.bfloat16)
                out_copy(dst, c, 2 * pair).start()

        for k in range(1, flight):
            recv_out[2 * other_pair(k) + 1, c] = jnp.zeros((PACK, out_half), recv_out.dtype)

    for c in list(range(RELAY_OUT, OUT_CHUNKS)) + list(range(RELAY_OUT)):
        lo = c * out_width
        out_copy(partner, c, partner).wait_recv()
        for k in range(1, flight):
            out_copy(partner, c, 2 * other_pair(k)).wait_recv()
            if c >= RELAY_OUT:
                out_copy(partner, c, 2 * other_pair(k) + 1).wait_recv()
        packed = recv_out[:, c].reshape(n * PACK, out_half)
        mixed = jnp.dot(combine, packed, preferred_element_type=jnp.float32).astype(jnp.bfloat16)
        out_ref[:, lo : lo + out_half] = mixed[:tokens]
        out_ref[:, lo + out_half : lo + out_width] = mixed[tokens:]

    for c in range(IN_CHUNKS):
        for dst in row_targets(c):
            row_copy(dst, c).wait_send()
        if c < RELAY_IN:
            for src in others():

                @pl.when(near_of(src, pair) == me)
                def _():
                    relay_copy(src, c).wait_send()

    for c in range(OUT_CHUNKS):
        for dst in others():
            out_copy(dst, c, me).wait_send()
        out_copy(partner, c, me).wait_send()


def body(tokens, expert_ids, gates, weights_in, weights_out):
    n = lax.axis_size("expert")
    flight = n // 2
    local, width = tokens.shape
    hid = weights_out.shape[1]
    in_half = width // IN_CHUNKS // 2
    out_half = width // OUT_CHUNKS // 2
    dtype = tokens.dtype
    return pl.pallas_call(
        partial(kernel, n),
        out_shape=pltpu.VMEM((local, width), dtype),
        in_specs=[pl.BlockSpec(memory_space=pltpu.HBM)] * 5,
        out_specs=pl.BlockSpec(memory_space=pltpu.VMEM),
        scratch_shapes=[
            pltpu.VMEM((local, width), dtype),
            pltpu.VMEM(expert_ids.shape[::-1], expert_ids.dtype),
            pltpu.VMEM(gates.shape[::-1], gates.dtype),
            pltpu.VMEM(weights_in.shape[1:], weights_in.dtype),
            pltpu.VMEM(weights_out.shape[1:], weights_out.dtype),
            pltpu.VMEM((flight, IN_CHUNKS, PACK, in_half), dtype),
            pltpu.VMEM((n, IN_CHUNKS, PACK, in_half), dtype),
            pltpu.VMEM((n, OUT_CHUNKS, PACK, out_half), dtype),
            pltpu.VMEM((n, OUT_CHUNKS, PACK, out_half), dtype),
            pltpu.VMEM((n, max(RELAY_OUT, 1), PACK, out_half), dtype),
            pltpu.SemaphoreType.DMA((3,)),
            pltpu.SemaphoreType.DMA((IN_CHUNKS,)),
            pltpu.SemaphoreType.DMA,
            pltpu.SemaphoreType.DMA((n, IN_CHUNKS)),
            pltpu.SemaphoreType.DMA((n, IN_CHUNKS)),
            pltpu.SemaphoreType.DMA((n, OUT_CHUNKS)),
            pltpu.SemaphoreType.DMA((n, OUT_CHUNKS)),
            pltpu.SemaphoreType.DMA((n, IN_CHUNKS)),
            pltpu.SemaphoreType.DMA((n, OUT_CHUNKS)),
        ],
        compiler_params=pltpu.CompilerParams(
            collective_id=0, has_side_effects=True, vmem_limit_bytes=56 * 2**20
        ),
    )(tokens, expert_ids.T, gates.T, weights_in, weights_out)


def solution(mesh):
    return jax.shard_map(
        body,
        mesh=mesh,
        in_specs=(
            P(("dp", "expert"), None),
            P(("dp", "expert"), None),
            P(("dp", "expert"), None),
            P("expert", None, None),
            P("expert", None, None),
        ),
        out_specs=P(("dp", "expert"), None),
        check_vma=False,
    )
```

```python
from functools import partial

import jax
import jax.numpy as jnp
from jax import lax
from jax.experimental import pallas as pl
from jax.experimental.pallas import tpu as pltpu
from jax.sharding import PartitionSpec as P

SRC_CAP = 8
PACK = 2 * SRC_CAP
IN_CHUNKS = 2
OUT_CHUNKS = 2
RELAY_IN = 0
RELAY_OUT = 0
MESH = pl.DeviceIdType.MESH


def slot_matrix(value, routed, position, rows, rows_per_expert):
    tokens = value[0].shape[1]
    row = lax.broadcasted_iota(jnp.int32, (rows, tokens), 0)
    slot = (row % SRC_CAP).astype(jnp.float32)
    expert = row // rows_per_expert
    table = jnp.zeros((rows, tokens), jnp.float32)
    for e in range(len(value)):
        hit = (expert == e) & (position[e] == slot) & (routed[e] > 0.0)
        table = jnp.where(hit, value[e], table)
    return table


def split_halves(table, axis):
    half = (lax.broadcasted_iota(jnp.int32, table.shape, axis) // SRC_CAP) % 2
    zero = jnp.zeros_like(table)
    return jnp.where(half == 0, table, zero), jnp.where(half == 1, table, zero)


def kernel(
    n,
    tok_hbm,
    ids_hbm,
    gate_hbm,
    win_hbm,
    wout_hbm,
    out_ref,
    tok,
    ids,
    gate,
    win,
    wout,
    send_rows,
    recv_rows,
    send_out,
    recv_out,
    partial_out,
    small_sem,
    win_sem,
    wout_sem,
    row_send_sem,
    row_recv_sem,
    out_send_sem,
    out_recv_sem,
    relay_sem,
    partial_sem,
):
    me = lax.axis_index("expert")
    flight = n // 2
    width = tok.shape[1]
    hid = wout.shape[0]
    in_width = width // IN_CHUNKS
    in_half = in_width // 2
    out_width = width // OUT_CHUNKS
    out_half = out_width // 2

    pair = me // 2
    partner = me + 1 - 2 * (me % 2)

    def peer(d):
        return lax.rem(me + d, n)

    def other_pair(k):
        return lax.rem(pair + k, flight)

    def near_of(source, target_pair):
        return 2 * target_pair + jnp.where(source < 2 * target_pair, 0, 1)

    def others():
        for k in range(1, flight):
            for member in range(2):
                yield 2 * other_pair(k) + member

    barrier = pltpu.get_barrier_semaphore()
    for d in range(1, n):
        pl.semaphore_signal(barrier, inc=1, device_id={"expert": peer(d)}, device_id_type=MESH)

    small = [
        pltpu.make_async_copy(ids_hbm, ids, small_sem.at[0]),
        pltpu.make_async_copy(gate_hbm, gate, small_sem.at[1]),
        pltpu.make_async_copy(tok_hbm, tok, small_sem.at[2]),
    ]
    for copy in small:
        copy.start()

    def win_copy(c):
        rows = pl.ds(c * in_width, in_width)
        return pltpu.make_async_copy(win_hbm.at[0, rows], win.at[rows], win_sem.at[c])

    wout_copy = pltpu.make_async_copy(wout_hbm.at[0], wout, wout_sem)
    for c in range(IN_CHUNKS):
        win_copy(c).start()
    wout_copy.start()

    small[0].wait()
    small[1].wait()
    chosen = ids[...]
    gates = gate[...].astype(jnp.float32)
    tokens = chosen.shape[1]
    weight, routed = [], []
    for e in range(flight):
        match = chosen == e
        weight.append(jnp.sum(jnp.where(match, gates, 0.0), axis=0, keepdims=True))
        routed.append(jnp.sum(jnp.where(match, 1.0, 0.0), axis=0, keepdims=True))
    row = lax.broadcasted_iota(jnp.int32, (PACK, tokens), 0)
    marks = jnp.zeros((PACK, tokens), jnp.float32)
    for e in range(flight):
        marks = jnp.where(row == e, routed[e], marks)
    before = lax.broadcasted_iota(jnp.int32, (tokens, tokens), 0) < lax.broadcasted_iota(
        jnp.int32, (tokens, tokens), 1
    )
    ahead = jnp.dot(
        marks.astype(jnp.bfloat16),
        before.astype(jnp.float32).astype(jnp.bfloat16),
        preferred_element_type=jnp.float32,
    )
    position = [ahead[e : e + 1] for e in range(flight)]
    pick = slot_matrix(routed, routed, position, flight * PACK, PACK)
    pick = [part.astype(jnp.bfloat16) for part in split_halves(pick, 0)]

    def row_copy(dst, c):
        return pltpu.make_async_remote_copy(
            src_ref=send_rows.at[dst // 2, c],
            dst_ref=recv_rows.at[me, c],
            send_sem=row_send_sem.at[dst, c],
            recv_sem=row_recv_sem.at[me, c],
            device_id={"expert": dst},
            device_id_type=MESH,
        )

    def relay_copy(src, c):
        return pltpu.make_async_remote_copy(
            src_ref=recv_rows.at[src, c],
            dst_ref=recv_rows.at[src, c],
            send_sem=relay_sem.at[src, c],
            recv_sem=row_recv_sem.at[src, c],
            device_id={"expert": partner},
            device_id_type=MESH,
        )

    def row_targets(c):
        for k in range(1, flight):
            near = near_of(me, other_pair(k))
            yield near
            if c >= RELAY_IN:
                yield 4 * other_pair(k) + 1 - near
        yield partner

    small[2].wait()
    for c in range(IN_CHUNKS):
        lo = c * in_width
        rows = sum(
            jnp.dot(
                pick[half],
                tok[:, lo + half * in_half : lo + (half + 1) * in_half],
                preferred_element_type=jnp.float32,
            )
            for half in range(2)
        ).astype(jnp.bfloat16)
        send_rows[:, c] = rows.reshape(flight, PACK, in_half)
        if c == 0:
            pl.semaphore_wait(barrier, n - 1)
        for dst in row_targets(c):
            row_copy(dst, c).start()
        recv_rows[me, c] = send_rows[me // 2, c]

    combine = jnp.transpose(slot_matrix(weight, routed, position, n * PACK, 2 * PACK))
    combine = jnp.concatenate(split_halves(combine, 1), axis=0).astype(jnp.bfloat16)

    def in_step(c, total):
        win_copy(c).wait()
        for src in others():
            relay_copy(src, c).wait_recv()

            @pl.when((near_of(src, pair) == me) & (c < RELAY_IN))
            def _():
                relay_copy(src, c).start()

        relay_copy(partner, c).wait_recv()
        packed = recv_rows[:, c].astype(jnp.float32)
        for half in range(2):
            rows = packed[:, half * SRC_CAP : (half + 1) * SRC_CAP].reshape(n * SRC_CAP, in_half)
            start = pl.multiple_of(c * in_width + half * in_half, in_half)
            total = total + jnp.dot(
                rows.astype(jnp.bfloat16),
                win[pl.ds(start, in_half)],
                preferred_element_type=jnp.float32,
            )
        return total

    merged = lax.fori_loop(
        0, IN_CHUNKS, in_step, jnp.zeros((n * SRC_CAP, 2 * hid), jnp.float32)
    )
    left = merged[:, :hid]
    hidden = (left / (1.0 + jnp.exp(-left)) * merged[:, hid:]).astype(jnp.bfloat16)

    def out_copy(dst, c, slot):
        return pltpu.make_async_remote_copy(
            src_ref=send_out.at[dst, c],
            dst_ref=recv_out.at[slot, c],
            send_sem=out_send_sem.at[dst, c],
            recv_sem=out_recv_sem.at[slot, c],
            device_id={"expert": dst},
            device_id_type=MESH,
        )

    def partial_copy(dst, c):
        return pltpu.make_async_remote_copy(
            src_ref=send_out.at[dst, c],
            dst_ref=partial_out.at[dst, c],
            send_sem=out_send_sem.at[dst, c],
            recv_sem=partial_sem.at[dst, c],
            device_id={"expert": partner},
            device_id_type=MESH,
        )

    wout_copy.wait()
    for c in range(OUT_CHUNKS):
        lo = c * out_width
        output = jnp.dot(
            hidden, wout[:, lo : lo + out_width], preferred_element_type=jnp.float32
        ).reshape(n, SRC_CAP, out_width)
        packed = jnp.concatenate([output[:, :, :out_half], output[:, :, out_half:]], axis=1)
        send_out[:, c] = packed.astype(jnp.bfloat16)
        for dst in others():
            if c < RELAY_OUT:

                @pl.when(near_of(dst, pair) != me)
                def _():
                    partial_copy(dst, c).start()
            else:
                out_copy(dst, c, me).start()
        out_copy(partner, c, me).start()
        recv_out[me, c] = send_out[me, c]

    for c in range(RELAY_OUT):
        for dst in others():

            @pl.when(near_of(dst, pair) == me)
            def _():
                partial_copy(dst, c).wait_recv()
                both = send_out[dst, c].astype(jnp.float32) + partial_out[dst, c].astype(
                    jnp.float32
                )
                send_out[dst, c] = both.astype(jnp.bfloat16)
                out_copy(dst, c, 2 * pair).start()

        for k in range(1, flight):
            recv_out[2 * other_pair(k) + 1, c] = jnp.zeros((PACK, out_half), recv_out.dtype)

    for c in list(range(RELAY_OUT, OUT_CHUNKS)) + list(range(RELAY_OUT)):
        lo = c * out_width
        out_copy(partner, c, partner).wait_recv()
        for k in range(1, flight):
            out_copy(partner, c, 2 * other_pair(k)).wait_recv()
            if c >= RELAY_OUT:
                out_copy(partner, c, 2 * other_pair(k) + 1).wait_recv()
        packed = recv_out[:, c].reshape(n * PACK, out_half)
        mixed = jnp.dot(combine, packed, preferred_element_type=jnp.float32).astype(jnp.bfloat16)
        out_ref[:, lo : lo + out_half] = mixed[:tokens]
        out_ref[:, lo + out_half : lo + out_width] = mixed[tokens:]

    for c in range(IN_CHUNKS):
        for dst in row_targets(c):
            row_copy(dst, c).wait_send()
        if c < RELAY_IN:
            for src in others():

                @pl.when(near_of(src, pair) == me)
                def _():
                    relay_copy(src, c).wait_send()

    for c in range(OUT_CHUNKS):
        for dst in others():
            out_copy(dst, c, me).wait_send()
        out_copy(partner, c, me).wait_send()


def body(tokens, expert_ids, gates, weights_in, weights_out):
    n = lax.axis_size("expert")
    flight = n // 2
    local, width = tokens.shape
    hid = weights_out.shape[1]
    in_half = width // IN_CHUNKS // 2
    out_half = width // OUT_CHUNKS // 2
    dtype = tokens.dtype
    return pl.pallas_call(
        partial(kernel, n),
        out_shape=pltpu.VMEM((local, width), dtype),
        in_specs=[pl.BlockSpec(memory_space=pltpu.HBM)] * 5,
        out_specs=pl.BlockSpec(memory_space=pltpu.VMEM),
        scratch_shapes=[
            pltpu.VMEM((local, width), dtype),
            pltpu.VMEM(expert_ids.shape[::-1], expert_ids.dtype),
            pltpu.VMEM(gates.shape[::-1], gates.dtype),
            pltpu.VMEM(weights_in.shape[1:], weights_in.dtype),
            pltpu.VMEM(weights_out.shape[1:], weights_out.dtype),
            pltpu.VMEM((flight, IN_CHUNKS, PACK, in_half), dtype),
            pltpu.VMEM((n, IN_CHUNKS, PACK, in_half), dtype),
            pltpu.VMEM((n, OUT_CHUNKS, PACK, out_half), dtype),
            pltpu.VMEM((n, OUT_CHUNKS, PACK, out_half), dtype),
            pltpu.VMEM((n, max(RELAY_OUT, 1), PACK, out_half), dtype),
            pltpu.SemaphoreType.DMA((3,)),
            pltpu.SemaphoreType.DMA((IN_CHUNKS,)),
            pltpu.SemaphoreType.DMA,
            pltpu.SemaphoreType.DMA((n, IN_CHUNKS)),
            pltpu.SemaphoreType.DMA((n, IN_CHUNKS)),
            pltpu.SemaphoreType.DMA((n, OUT_CHUNKS)),
            pltpu.SemaphoreType.DMA((n, OUT_CHUNKS)),
            pltpu.SemaphoreType.DMA((n, IN_CHUNKS)),
            pltpu.SemaphoreType.DMA((n, OUT_CHUNKS)),
        ],
        compiler_params=pltpu.CompilerParams(
            collective_id=0, has_side_effects=True, vmem_limit_bytes=56 * 2**20
        ),
    )(tokens, expert_ids.T, gates.T, weights_in, weights_out)


def solution(mesh):
    return jax.shard_map(
        body,
        mesh=mesh,
        in_specs=(
            P(("dp", "expert"), None),
            P(("dp", "expert"), None),
            P(("dp", "expert"), None),
            P("expert", None, None),
            P("expert", None, None),
        ),
        out_specs=P(("dp", "expert"), None),
        check_vma=False,
    )
```

```python
from functools import partial

import jax
import jax.numpy as jnp
from jax import lax
from jax.experimental import pallas as pl
from jax.experimental.pallas import tpu as pltpu
from jax.sharding import PartitionSpec as P

SRC_CAP = 8
PACK = 2 * SRC_CAP
IN_CHUNKS = 4
IN_FLIGHT = 2
OUT_CHUNKS = 2
RELAY_IN = 0
RELAY_OUT = 0
MESH = pl.DeviceIdType.MESH


def slot_matrix(value, routed, position, rows, rows_per_expert):
    tokens = value[0].shape[1]
    row = lax.broadcasted_iota(jnp.int32, (rows, tokens), 0)
    slot = (row % SRC_CAP).astype(jnp.float32)
    expert = row // rows_per_expert
    table = jnp.zeros((rows, tokens), jnp.float32)
    for e in range(len(value)):
        hit = (expert == e) & (position[e] == slot) & (routed[e] > 0.0)
        table = jnp.where(hit, value[e], table)
    return table


def split_halves(table, axis):
    half = (lax.broadcasted_iota(jnp.int32, table.shape, axis) // SRC_CAP) % 2
    zero = jnp.zeros_like(table)
    return jnp.where(half == 0, table, zero), jnp.where(half == 1, table, zero)


def kernel(
    n,
    tok_hbm,
    ids_hbm,
    gate_hbm,
    win_hbm,
    wout_hbm,
    out_ref,
    tok,
    ids,
    gate,
    win,
    wout,
    send_rows,
    recv_rows,
    send_out,
    recv_out,
    partial_out,
    small_sem,
    win_sem,
    wout_sem,
    row_send_sem,
    row_recv_sem,
    out_send_sem,
    out_recv_sem,
    relay_sem,
    partial_sem,
):
    me = lax.axis_index("expert")
    flight = n // 2
    width = tok.shape[1]
    hid = wout.shape[0]
    in_width = width // IN_CHUNKS
    in_half = in_width // 2
    out_width = width // OUT_CHUNKS
    out_half = out_width // 2

    pair = me // 2
    partner = me + 1 - 2 * (me % 2)

    def peer(d):
        return lax.rem(me + d, n)

    def other_pair(k):
        return lax.rem(pair + k, flight)

    def near_of(source, target_pair):
        return 2 * target_pair + jnp.where(source < 2 * target_pair, 0, 1)

    def others():
        for k in range(1, flight):
            for member in range(2):
                yield 2 * other_pair(k) + member

    barrier = pltpu.get_barrier_semaphore()
    for d in range(1, n):
        pl.semaphore_signal(barrier, inc=1, device_id={"expert": peer(d)}, device_id_type=MESH)

    small = [
        pltpu.make_async_copy(ids_hbm, ids, small_sem.at[0]),
        pltpu.make_async_copy(gate_hbm, gate, small_sem.at[1]),
        pltpu.make_async_copy(tok_hbm, tok, small_sem.at[2]),
    ]
    for copy in small:
        copy.start()

    def win_copy(c):
        rows = pl.ds(c * in_width, in_width)
        return pltpu.make_async_copy(win_hbm.at[0, rows], win.at[rows], win_sem.at[c])

    wout_copy = pltpu.make_async_copy(wout_hbm.at[0], wout, wout_sem)
    for c in range(IN_CHUNKS):
        win_copy(c).start()
    wout_copy.start()

    small[0].wait()
    small[1].wait()
    chosen = ids[...]
    gates = gate[...].astype(jnp.float32)
    tokens = chosen.shape[1]
    weight, routed = [], []
    for e in range(flight):
        match = chosen == e
        weight.append(jnp.sum(jnp.where(match, gates, 0.0), axis=0, keepdims=True))
        routed.append(jnp.sum(jnp.where(match, 1.0, 0.0), axis=0, keepdims=True))
    row = lax.broadcasted_iota(jnp.int32, (PACK, tokens), 0)
    marks = jnp.zeros((PACK, tokens), jnp.float32)
    for e in range(flight):
        marks = jnp.where(row == e, routed[e], marks)
    before = lax.broadcasted_iota(jnp.int32, (tokens, tokens), 0) < lax.broadcasted_iota(
        jnp.int32, (tokens, tokens), 1
    )
    ahead = jnp.dot(
        marks.astype(jnp.bfloat16),
        before.astype(jnp.float32).astype(jnp.bfloat16),
        preferred_element_type=jnp.float32,
    )
    position = [ahead[e : e + 1] for e in range(flight)]
    pick = slot_matrix(routed, routed, position, flight * PACK, PACK)
    pick = [part.astype(jnp.bfloat16) for part in split_halves(pick, 0)]

    def row_copy(dst, c):
        return pltpu.make_async_remote_copy(
            src_ref=send_rows.at[dst // 2, c],
            dst_ref=recv_rows.at[me, c],
            send_sem=row_send_sem.at[dst, c],
            recv_sem=row_recv_sem.at[me, c],
            device_id={"expert": dst},
            device_id_type=MESH,
        )

    def relay_copy(src, c):
        return pltpu.make_async_remote_copy(
            src_ref=recv_rows.at[src, c],
            dst_ref=recv_rows.at[src, c],
            send_sem=relay_sem.at[src, c],
            recv_sem=row_recv_sem.at[src, c],
            device_id={"expert": partner},
            device_id_type=MESH,
        )

    def row_targets(c):
        for k in range(1, flight):
            near = near_of(me, other_pair(k))
            yield near
            if c >= RELAY_IN:
                yield 4 * other_pair(k) + 1 - near
        yield partner

    small[2].wait()
    for c in range(IN_CHUNKS):
        lo = c * in_width
        rows = sum(
            jnp.dot(
                pick[half],
                tok[:, lo + half * in_half : lo + (half + 1) * in_half],
                preferred_element_type=jnp.float32,
            )
            for half in range(2)
        ).astype(jnp.bfloat16)
        send_rows[:, c] = rows.reshape(flight, PACK, in_half)
        if c == 0:
            pl.semaphore_wait(barrier, n - 1)
        if c >= IN_FLIGHT:
            for dst in row_targets(c - IN_FLIGHT):
                row_copy(dst, c - IN_FLIGHT).wait_send()
        for dst in row_targets(c):
            row_copy(dst, c).start()
        recv_rows[me, c] = send_rows[me // 2, c]

    combine = jnp.transpose(slot_matrix(weight, routed, position, n * PACK, 2 * PACK))
    combine = jnp.concatenate(split_halves(combine, 1), axis=0).astype(jnp.bfloat16)

    def in_step(c, total):
        win_copy(c).wait()
        for src in others():
            relay_copy(src, c).wait_recv()

            @pl.when((near_of(src, pair) == me) & (c < RELAY_IN))
            def _():
                relay_copy(src, c).start()

        relay_copy(partner, c).wait_recv()
        packed = recv_rows[:, c].astype(jnp.float32)
        for half in range(2):
            rows = packed[:, half * SRC_CAP : (half + 1) * SRC_CAP].reshape(n * SRC_CAP, in_half)
            start = pl.multiple_of(c * in_width + half * in_half, in_half)
            total = total + jnp.dot(
                rows.astype(jnp.bfloat16),
                win[pl.ds(start, in_half)],
                preferred_element_type=jnp.float32,
            )
        return total

    merged = lax.fori_loop(
        0, IN_CHUNKS, in_step, jnp.zeros((n * SRC_CAP, 2 * hid), jnp.float32)
    )
    left = merged[:, :hid]
    hidden = (left / (1.0 + jnp.exp(-left)) * merged[:, hid:]).astype(jnp.bfloat16)

    def out_copy(dst, c, slot):
        return pltpu.make_async_remote_copy(
            src_ref=send_out.at[dst, c],
            dst_ref=recv_out.at[slot, c],
            send_sem=out_send_sem.at[dst, c],
            recv_sem=out_recv_sem.at[slot, c],
            device_id={"expert": dst},
            device_id_type=MESH,
        )

    def partial_copy(dst, c):
        return pltpu.make_async_remote_copy(
            src_ref=send_out.at[dst, c],
            dst_ref=partial_out.at[dst, c],
            send_sem=out_send_sem.at[dst, c],
            recv_sem=partial_sem.at[dst, c],
            device_id={"expert": partner},
            device_id_type=MESH,
        )

    wout_copy.wait()
    for c in range(OUT_CHUNKS):
        lo = c * out_width
        output = jnp.dot(
            hidden, wout[:, lo : lo + out_width], preferred_element_type=jnp.float32
        ).reshape(n, SRC_CAP, out_width)
        packed = jnp.concatenate([output[:, :, :out_half], output[:, :, out_half:]], axis=1)
        send_out[:, c] = packed.astype(jnp.bfloat16)
        for dst in others():
            if c < RELAY_OUT:

                @pl.when(near_of(dst, pair) != me)
                def _():
                    partial_copy(dst, c).start()
            else:
                out_copy(dst, c, me).start()
        out_copy(partner, c, me).start()
        recv_out[me, c] = send_out[me, c]

    for c in range(RELAY_OUT):
        for dst in others():

            @pl.when(near_of(dst, pair) == me)
            def _():
                partial_copy(dst, c).wait_recv()
                both = send_out[dst, c].astype(jnp.float32) + partial_out[dst, c].astype(
                    jnp.float32
                )
                send_out[dst, c] = both.astype(jnp.bfloat16)
                out_copy(dst, c, 2 * pair).start()

        for k in range(1, flight):
            recv_out[2 * other_pair(k) + 1, c] = jnp.zeros((PACK, out_half), recv_out.dtype)

    for c in list(range(RELAY_OUT, OUT_CHUNKS)) + list(range(RELAY_OUT)):
        lo = c * out_width
        out_copy(partner, c, partner).wait_recv()
        for k in range(1, flight):
            out_copy(partner, c, 2 * other_pair(k)).wait_recv()
            if c >= RELAY_OUT:
                out_copy(partner, c, 2 * other_pair(k) + 1).wait_recv()
        packed = recv_out[:, c].reshape(n * PACK, out_half)
        mixed = jnp.dot(combine, packed, preferred_element_type=jnp.float32).astype(jnp.bfloat16)
        out_ref[:, lo : lo + out_half] = mixed[:tokens]
        out_ref[:, lo + out_half : lo + out_width] = mixed[tokens:]

    for c in range(IN_CHUNKS):
        if c >= IN_CHUNKS - IN_FLIGHT:
            for dst in row_targets(c):
                row_copy(dst, c).wait_send()
        if c < RELAY_IN:
            for src in others():

                @pl.when(near_of(src, pair) == me)
                def _():
                    relay_copy(src, c).wait_send()

    for c in range(OUT_CHUNKS):
        for dst in others():
            out_copy(dst, c, me).wait_send()
        out_copy(partner, c, me).wait_send()


def body(tokens, expert_ids, gates, weights_in, weights_out):
    n = lax.axis_size("expert")
    flight = n // 2
    local, width = tokens.shape
    hid = weights_out.shape[1]
    in_half = width // IN_CHUNKS // 2
    out_half = width // OUT_CHUNKS // 2
    dtype = tokens.dtype
    return pl.pallas_call(
        partial(kernel, n),
        out_shape=pltpu.VMEM((local, width), dtype),
        in_specs=[pl.BlockSpec(memory_space=pltpu.HBM)] * 5,
        out_specs=pl.BlockSpec(memory_space=pltpu.VMEM),
        scratch_shapes=[
            pltpu.VMEM((local, width), dtype),
            pltpu.VMEM(expert_ids.shape[::-1], expert_ids.dtype),
            pltpu.VMEM(gates.shape[::-1], gates.dtype),
            pltpu.VMEM(weights_in.shape[1:], weights_in.dtype),
            pltpu.VMEM(weights_out.shape[1:], weights_out.dtype),
            pltpu.VMEM((flight, IN_CHUNKS, PACK, in_half), dtype),
            pltpu.VMEM((n, IN_CHUNKS, PACK, in_half), dtype),
            pltpu.VMEM((n, OUT_CHUNKS, PACK, out_half), dtype),
            pltpu.VMEM((n, OUT_CHUNKS, PACK, out_half), dtype),
            pltpu.VMEM((n, max(RELAY_OUT, 1), PACK, out_half), dtype),
            pltpu.SemaphoreType.DMA((3,)),
            pltpu.SemaphoreType.DMA((IN_CHUNKS,)),
            pltpu.SemaphoreType.DMA,
            pltpu.SemaphoreType.DMA((n, IN_CHUNKS)),
            pltpu.SemaphoreType.DMA((n, IN_CHUNKS)),
            pltpu.SemaphoreType.DMA((n, OUT_CHUNKS)),
            pltpu.SemaphoreType.DMA((n, OUT_CHUNKS)),
            pltpu.SemaphoreType.DMA((n, IN_CHUNKS)),
            pltpu.SemaphoreType.DMA((n, OUT_CHUNKS)),
        ],
        compiler_params=pltpu.CompilerParams(
            collective_id=0, has_side_effects=True, vmem_limit_bytes=56 * 2**20
        ),
    )(tokens, expert_ids.T, gates.T, weights_in, weights_out)


def solution(mesh):
    return jax.shard_map(
        body,
        mesh=mesh,
        in_specs=(
            P(("dp", "expert"), None),
            P(("dp", "expert"), None),
            P(("dp", "expert"), None),
            P("expert", None, None),
            P("expert", None, None),
        ),
        out_specs=P(("dp", "expert"), None),
        check_vma=False,
    )
```

```python
from functools import partial

import jax
import jax.numpy as jnp
from jax import lax
from jax.experimental import pallas as pl
from jax.experimental.pallas import tpu as pltpu
from jax.sharding import PartitionSpec as P

SRC_CAP = 8
PACK = 2 * SRC_CAP
IN_CHUNKS = 2
OUT_CHUNKS = 2
RELAY_IN = 1
RELAY_OUT = 0
MESH = pl.DeviceIdType.MESH


def slot_matrix(value, routed, position, rows, rows_per_expert):
    tokens = value[0].shape[1]
    row = lax.broadcasted_iota(jnp.int32, (rows, tokens), 0)
    slot = (row % SRC_CAP).astype(jnp.float32)
    expert = row // rows_per_expert
    table = jnp.zeros((rows, tokens), jnp.float32)
    for e in range(len(value)):
        hit = (expert == e) & (position[e] == slot) & (routed[e] > 0.0)
        table = jnp.where(hit, value[e], table)
    return table


def split_halves(table, axis):
    half = (lax.broadcasted_iota(jnp.int32, table.shape, axis) // SRC_CAP) % 2
    zero = jnp.zeros_like(table)
    return jnp.where(half == 0, table, zero), jnp.where(half == 1, table, zero)


def kernel(
    n,
    tok_hbm,
    ids_hbm,
    gate_hbm,
    win_hbm,
    wout_hbm,
    out_ref,
    tok,
    ids,
    gate,
    win,
    wout,
    send_rows,
    recv_rows,
    send_out,
    recv_out,
    partial_out,
    small_sem,
    win_sem,
    wout_sem,
    row_send_sem,
    row_recv_sem,
    out_send_sem,
    out_recv_sem,
    relay_sem,
    partial_sem,
):
    me = lax.axis_index("expert")
    flight = n // 2
    width = tok.shape[1]
    hid = wout.shape[0]
    in_width = width // IN_CHUNKS
    in_half = in_width // 2
    out_width = width // OUT_CHUNKS
    out_half = out_width // 2

    pair = me // 2
    partner = me + 1 - 2 * (me % 2)

    def peer(d):
        return lax.rem(me + d, n)

    def other_pair(k):
        return lax.rem(pair + k, flight)

    def near_of(source, target_pair):
        return 2 * target_pair + jnp.where(source < 2 * target_pair, 0, 1)

    def others():
        for k in range(1, flight):
            for member in range(2):
                yield 2 * other_pair(k) + member

    barrier = pltpu.get_barrier_semaphore()
    for d in range(1, n):
        pl.semaphore_signal(barrier, inc=1, device_id={"expert": peer(d)}, device_id_type=MESH)

    small = [
        pltpu.make_async_copy(ids_hbm, ids, small_sem.at[0]),
        pltpu.make_async_copy(gate_hbm, gate, small_sem.at[1]),
        pltpu.make_async_copy(tok_hbm, tok, small_sem.at[2]),
    ]
    for copy in small:
        copy.start()

    def win_copy(c):
        rows = pl.ds(c * in_width, in_width)
        return pltpu.make_async_copy(win_hbm.at[0, rows], win.at[rows], win_sem.at[c])

    wout_copy = pltpu.make_async_copy(wout_hbm.at[0], wout, wout_sem)
    for c in range(IN_CHUNKS):
        win_copy(c).start()
    wout_copy.start()

    small[0].wait()
    small[1].wait()
    chosen = ids[...]
    gates = gate[...].astype(jnp.float32)
    tokens = chosen.shape[1]
    weight, routed = [], []
    for e in range(flight):
        match = chosen == e
        weight.append(jnp.sum(jnp.where(match, gates, 0.0), axis=0, keepdims=True))
        routed.append(jnp.sum(jnp.where(match, 1.0, 0.0), axis=0, keepdims=True))
    row = lax.broadcasted_iota(jnp.int32, (PACK, tokens), 0)
    marks = jnp.zeros((PACK, tokens), jnp.float32)
    for e in range(flight):
        marks = jnp.where(row == e, routed[e], marks)
    before = lax.broadcasted_iota(jnp.int32, (tokens, tokens), 0) < lax.broadcasted_iota(
        jnp.int32, (tokens, tokens), 1
    )
    ahead = jnp.dot(
        marks.astype(jnp.bfloat16),
        before.astype(jnp.float32).astype(jnp.bfloat16),
        preferred_element_type=jnp.float32,
    )
    position = [ahead[e : e + 1] for e in range(flight)]
    pick = slot_matrix(routed, routed, position, flight * PACK, PACK)
    pick = [part.astype(jnp.bfloat16) for part in split_halves(pick, 0)]

    def row_copy(dst, c):
        return pltpu.make_async_remote_copy(
            src_ref=send_rows.at[dst // 2, c],
            dst_ref=recv_rows.at[me, c],
            send_sem=row_send_sem.at[dst, c],
            recv_sem=row_recv_sem.at[me, c],
            device_id={"expert": dst},
            device_id_type=MESH,
        )

    def relay_copy(src, c):
        return pltpu.make_async_remote_copy(
            src_ref=recv_rows.at[src, c],
            dst_ref=recv_rows.at[src, c],
            send_sem=relay_sem.at[src, c],
            recv_sem=row_recv_sem.at[src, c],
            device_id={"expert": partner},
            device_id_type=MESH,
        )

    def row_targets(c):
        for k in range(1, flight):
            near = near_of(me, other_pair(k))
            yield near
            if c >= RELAY_IN:
                yield 4 * other_pair(k) + 1 - near
        yield partner

    small[2].wait()
    for c in range(IN_CHUNKS):
        lo = c * in_width
        rows = sum(
            jnp.dot(
                pick[half],
                tok[:, lo + half * in_half : lo + (half + 1) * in_half],
                preferred_element_type=jnp.float32,
            )
            for half in range(2)
        ).astype(jnp.bfloat16)
        send_rows[:, c] = rows.reshape(flight, PACK, in_half)
        if c == 0:
            pl.semaphore_wait(barrier, n - 1)
        for dst in row_targets(c):
            row_copy(dst, c).start()
        recv_rows[me, c] = send_rows[me // 2, c]

    combine = jnp.transpose(slot_matrix(weight, routed, position, n * PACK, 2 * PACK))
    combine = jnp.concatenate(split_halves(combine, 1), axis=0).astype(jnp.bfloat16)

    outer = (me % 2 == 0) == (2 * pair < flight)

    def in_step(step, total):
        c = jnp.where(outer, IN_CHUNKS - 1 - step, step)
        for src in others():
            relay_copy(src, c).wait_recv()

            @pl.when((near_of(src, pair) == me) & (c < RELAY_IN))
            def _():
                relay_copy(src, c).start()

        relay_copy(partner, c).wait_recv()
        win_copy(c).wait()
        packed = recv_rows[:, c].astype(jnp.float32)
        for half in range(2):
            rows = packed[:, half * SRC_CAP : (half + 1) * SRC_CAP].reshape(n * SRC_CAP, in_half)
            start = pl.multiple_of(c * in_width + half * in_half, in_half)
            total = total + jnp.dot(
                rows.astype(jnp.bfloat16),
                win[pl.ds(start, in_half)],
                preferred_element_type=jnp.float32,
            )
        return total

    merged = lax.fori_loop(
        0, IN_CHUNKS, in_step, jnp.zeros((n * SRC_CAP, 2 * hid), jnp.float32)
    )
    left = merged[:, :hid]
    hidden = (left / (1.0 + jnp.exp(-left)) * merged[:, hid:]).astype(jnp.bfloat16)

    def out_copy(dst, c, slot):
        return pltpu.make_async_remote_copy(
            src_ref=send_out.at[dst, c],
            dst_ref=recv_out.at[slot, c],
            send_sem=out_send_sem.at[dst, c],
            recv_sem=out_recv_sem.at[slot, c],
            device_id={"expert": dst},
            device_id_type=MESH,
        )

    def partial_copy(dst, c):
        return pltpu.make_async_remote_copy(
            src_ref=send_out.at[dst, c],
            dst_ref=partial_out.at[dst, c],
            send_sem=out_send_sem.at[dst, c],
            recv_sem=partial_sem.at[dst, c],
            device_id={"expert": partner},
            device_id_type=MESH,
        )

    wout_copy.wait()
    for c in range(OUT_CHUNKS):
        lo = c * out_width
        output = jnp.dot(
            hidden, wout[:, lo : lo + out_width], preferred_element_type=jnp.float32
        ).reshape(n, SRC_CAP, out_width)
        packed = jnp.concatenate([output[:, :, :out_half], output[:, :, out_half:]], axis=1)
        send_out[:, c] = packed.astype(jnp.bfloat16)
        for dst in others():
            if c < RELAY_OUT:

                @pl.when(near_of(dst, pair) != me)
                def _():
                    partial_copy(dst, c).start()
            else:
                out_copy(dst, c, me).start()
        out_copy(partner, c, me).start()
        recv_out[me, c] = send_out[me, c]

    for c in range(RELAY_OUT):
        for dst in others():

            @pl.when(near_of(dst, pair) == me)
            def _():
                partial_copy(dst, c).wait_recv()
                both = send_out[dst, c].astype(jnp.float32) + partial_out[dst, c].astype(
                    jnp.float32
                )
                send_out[dst, c] = both.astype(jnp.bfloat16)
                out_copy(dst, c, 2 * pair).start()

        for k in range(1, flight):
            recv_out[2 * other_pair(k) + 1, c] = jnp.zeros((PACK, out_half), recv_out.dtype)

    for c in list(range(RELAY_OUT, OUT_CHUNKS)) + list(range(RELAY_OUT)):
        lo = c * out_width
        out_copy(partner, c, partner).wait_recv()
        for k in range(1, flight):
            out_copy(partner, c, 2 * other_pair(k)).wait_recv()
            if c >= RELAY_OUT:
                out_copy(partner, c, 2 * other_pair(k) + 1).wait_recv()
        packed = recv_out[:, c].reshape(n * PACK, out_half)
        mixed = jnp.dot(combine, packed, preferred_element_type=jnp.float32).astype(jnp.bfloat16)
        out_ref[:, lo : lo + out_half] = mixed[:tokens]
        out_ref[:, lo + out_half : lo + out_width] = mixed[tokens:]

    for c in range(IN_CHUNKS):
        for dst in row_targets(c):
            row_copy(dst, c).wait_send()
        if c < RELAY_IN:
            for src in others():

                @pl.when(near_of(src, pair) == me)
                def _():
                    relay_copy(src, c).wait_send()

    for c in range(OUT_CHUNKS):
        for dst in others():
            out_copy(dst, c, me).wait_send()
        out_copy(partner, c, me).wait_send()


def body(tokens, expert_ids, gates, weights_in, weights_out):
    n = lax.axis_size("expert")
    flight = n // 2
    local, width = tokens.shape
    hid = weights_out.shape[1]
    in_half = width // IN_CHUNKS // 2
    out_half = width // OUT_CHUNKS // 2
    dtype = tokens.dtype
    return pl.pallas_call(
        partial(kernel, n),
        out_shape=pltpu.VMEM((local, width), dtype),
        in_specs=[pl.BlockSpec(memory_space=pltpu.HBM)] * 5,
        out_specs=pl.BlockSpec(memory_space=pltpu.VMEM),
        scratch_shapes=[
            pltpu.VMEM((local, width), dtype),
            pltpu.VMEM(expert_ids.shape[::-1], expert_ids.dtype),
            pltpu.VMEM(gates.shape[::-1], gates.dtype),
            pltpu.VMEM(weights_in.shape[1:], weights_in.dtype),
            pltpu.VMEM(weights_out.shape[1:], weights_out.dtype),
            pltpu.VMEM((flight, IN_CHUNKS, PACK, in_half), dtype),
            pltpu.VMEM((n, IN_CHUNKS, PACK, in_half), dtype),
            pltpu.VMEM((n, OUT_CHUNKS, PACK, out_half), dtype),
            pltpu.VMEM((n, OUT_CHUNKS, PACK, out_half), dtype),
            pltpu.VMEM((n, max(RELAY_OUT, 1), PACK, out_half), dtype),
            pltpu.SemaphoreType.DMA((3,)),
            pltpu.SemaphoreType.DMA((IN_CHUNKS,)),
            pltpu.SemaphoreType.DMA,
            pltpu.SemaphoreType.DMA((n, IN_CHUNKS)),
            pltpu.SemaphoreType.DMA((n, IN_CHUNKS)),
            pltpu.SemaphoreType.DMA((n, OUT_CHUNKS)),
            pltpu.SemaphoreType.DMA((n, OUT_CHUNKS)),
            pltpu.SemaphoreType.DMA((n, IN_CHUNKS)),
            pltpu.SemaphoreType.DMA((n, OUT_CHUNKS)),
        ],
        compiler_params=pltpu.CompilerParams(
            collective_id=0, has_side_effects=True, vmem_limit_bytes=56 * 2**20
        ),
    )(tokens, expert_ids.T, gates.T, weights_in, weights_out)


def solution(mesh):
    return jax.shard_map(
        body,
        mesh=mesh,
        in_specs=(
            P(("dp", "expert"), None),
            P(("dp", "expert"), None),
            P(("dp", "expert"), None),
            P("expert", None, None),
            P("expert", None, None),
        ),
        out_specs=P(("dp", "expert"), None),
        check_vma=False,
    )
```

```python
from functools import partial

import jax
import jax.numpy as jnp
from jax import lax
from jax.experimental import pallas as pl
from jax.experimental.pallas import tpu as pltpu
from jax.sharding import PartitionSpec as P

SRC_CAP = 8
PACK = 2 * SRC_CAP
IN_CHUNKS = 2
OUT_CHUNKS = 2
RELAY_IN = 1
RELAY_OUT = 1
MESH = pl.DeviceIdType.MESH


def slot_matrix(value, routed, position, rows, rows_per_expert):
    tokens = value[0].shape[1]
    row = lax.broadcasted_iota(jnp.int32, (rows, tokens), 0)
    slot = (row % SRC_CAP).astype(jnp.float32)
    expert = row // rows_per_expert
    table = jnp.zeros((rows, tokens), jnp.float32)
    for e in range(len(value)):
        hit = (expert == e) & (position[e] == slot) & (routed[e] > 0.0)
        table = jnp.where(hit, value[e], table)
    return table


def split_halves(table, axis):
    half = (lax.broadcasted_iota(jnp.int32, table.shape, axis) // SRC_CAP) % 2
    zero = jnp.zeros_like(table)
    return jnp.where(half == 0, table, zero), jnp.where(half == 1, table, zero)


def kernel(
    n,
    tok_hbm,
    ids_hbm,
    gate_hbm,
    win_hbm,
    wout_hbm,
    out_ref,
    tok,
    ids,
    gate,
    win,
    wout,
    send_rows,
    recv_rows,
    send_out,
    recv_out,
    partial_out,
    small_sem,
    win_sem,
    wout_sem,
    row_send_sem,
    row_recv_sem,
    out_send_sem,
    out_recv_sem,
    relay_sem,
    partial_sem,
):
    me = lax.axis_index("expert")
    flight = n // 2
    width = tok.shape[1]
    hid = wout.shape[0]
    in_width = width // IN_CHUNKS
    in_half = in_width // 2
    out_width = width // OUT_CHUNKS
    out_half = out_width // 2

    pair = me // 2
    partner = me + 1 - 2 * (me % 2)

    def peer(d):
        return lax.rem(me + d, n)

    def other_pair(k):
        return lax.rem(pair + k, flight)

    def near_of(source, target_pair):
        return 2 * target_pair + jnp.where(source < 2 * target_pair, 0, 1)

    def others():
        for k in range(1, flight):
            for member in range(2):
                yield 2 * other_pair(k) + member

    barrier = pltpu.get_barrier_semaphore()
    for d in range(1, n):
        pl.semaphore_signal(barrier, inc=1, device_id={"expert": peer(d)}, device_id_type=MESH)

    small = [
        pltpu.make_async_copy(ids_hbm, ids, small_sem.at[0]),
        pltpu.make_async_copy(gate_hbm, gate, small_sem.at[1]),
        pltpu.make_async_copy(tok_hbm, tok, small_sem.at[2]),
    ]
    for copy in small:
        copy.start()

    def win_copy(c):
        rows = pl.ds(c * in_width, in_width)
        return pltpu.make_async_copy(win_hbm.at[0, rows], win.at[rows], win_sem.at[c])

    wout_copy = pltpu.make_async_copy(wout_hbm.at[0], wout, wout_sem)
    for c in range(IN_CHUNKS):
        win_copy(c).start()
    wout_copy.start()

    small[0].wait()
    small[1].wait()
    chosen = ids[...]
    gates = gate[...].astype(jnp.float32)
    tokens = chosen.shape[1]
    weight, routed = [], []
    for e in range(flight):
        match = chosen == e
        weight.append(jnp.sum(jnp.where(match, gates, 0.0), axis=0, keepdims=True))
        routed.append(jnp.sum(jnp.where(match, 1.0, 0.0), axis=0, keepdims=True))
    row = lax.broadcasted_iota(jnp.int32, (PACK, tokens), 0)
    marks = jnp.zeros((PACK, tokens), jnp.float32)
    for e in range(flight):
        marks = jnp.where(row == e, routed[e], marks)
    before = lax.broadcasted_iota(jnp.int32, (tokens, tokens), 0) < lax.broadcasted_iota(
        jnp.int32, (tokens, tokens), 1
    )
    ahead = jnp.dot(
        marks.astype(jnp.bfloat16),
        before.astype(jnp.float32).astype(jnp.bfloat16),
        preferred_element_type=jnp.float32,
    )
    position = [ahead[e : e + 1] for e in range(flight)]
    pick = slot_matrix(routed, routed, position, flight * PACK, PACK)
    pick = [part.astype(jnp.bfloat16) for part in split_halves(pick, 0)]

    def row_copy(dst, c):
        return pltpu.make_async_remote_copy(
            src_ref=send_rows.at[dst // 2, c],
            dst_ref=recv_rows.at[me, c],
            send_sem=row_send_sem.at[dst, c],
            recv_sem=row_recv_sem.at[me, c],
            device_id={"expert": dst},
            device_id_type=MESH,
        )

    def relay_copy(src, c):
        return pltpu.make_async_remote_copy(
            src_ref=recv_rows.at[src, c],
            dst_ref=recv_rows.at[src, c],
            send_sem=relay_sem.at[src, c],
            recv_sem=row_recv_sem.at[src, c],
            device_id={"expert": partner},
            device_id_type=MESH,
        )

    def row_targets(c):
        for k in range(1, flight):
            near = near_of(me, other_pair(k))
            yield near
            if c >= RELAY_IN:
                yield 4 * other_pair(k) + 1 - near
        yield partner

    small[2].wait()
    for c in range(IN_CHUNKS):
        lo = c * in_width
        rows = sum(
            jnp.dot(
                pick[half],
                tok[:, lo + half * in_half : lo + (half + 1) * in_half],
                preferred_element_type=jnp.float32,
            )
            for half in range(2)
        ).astype(jnp.bfloat16)
        send_rows[:, c] = rows.reshape(flight, PACK, in_half)
        if c == 0:
            pl.semaphore_wait(barrier, n - 1)
        for dst in row_targets(c):
            row_copy(dst, c).start()
        recv_rows[me, c] = send_rows[me // 2, c]

    combine = jnp.transpose(slot_matrix(weight, routed, position, n * PACK, 2 * PACK))
    combine = jnp.concatenate(split_halves(combine, 1), axis=0).astype(jnp.bfloat16)

    outer = (me % 2 == 0) == (2 * pair < flight)

    def in_step(step, total):
        c = jnp.where(outer, IN_CHUNKS - 1 - step, step)
        for src in others():
            relay_copy(src, c).wait_recv()

            @pl.when((near_of(src, pair) == me) & (c < RELAY_IN))
            def _():
                relay_copy(src, c).start()

        relay_copy(partner, c).wait_recv()
        win_copy(c).wait()
        packed = recv_rows[:, c].astype(jnp.float32)
        for half in range(2):
            rows = packed[:, half * SRC_CAP : (half + 1) * SRC_CAP].reshape(n * SRC_CAP, in_half)
            start = pl.multiple_of(c * in_width + half * in_half, in_half)
            total = total + jnp.dot(
                rows.astype(jnp.bfloat16),
                win[pl.ds(start, in_half)],
                preferred_element_type=jnp.float32,
            )
        return total

    merged = lax.fori_loop(
        0, IN_CHUNKS, in_step, jnp.zeros((n * SRC_CAP, 2 * hid), jnp.float32)
    )
    left = merged[:, :hid]
    hidden = (left / (1.0 + jnp.exp(-left)) * merged[:, hid:]).astype(jnp.bfloat16)

    def out_copy(dst, c, slot):
        return pltpu.make_async_remote_copy(
            src_ref=send_out.at[dst, c],
            dst_ref=recv_out.at[slot, c],
            send_sem=out_send_sem.at[dst, c],
            recv_sem=out_recv_sem.at[slot, c],
            device_id={"expert": dst},
            device_id_type=MESH,
        )

    def partial_copy(dst, c):
        return pltpu.make_async_remote_copy(
            src_ref=send_out.at[dst, c],
            dst_ref=partial_out.at[dst, c],
            send_sem=out_send_sem.at[dst, c],
            recv_sem=partial_sem.at[dst, c],
            device_id={"expert": partner},
            device_id_type=MESH,
        )

    wout_copy.wait()
    for c in range(OUT_CHUNKS):
        lo = c * out_width
        output = jnp.dot(
            hidden, wout[:, lo : lo + out_width], preferred_element_type=jnp.float32
        ).reshape(n, SRC_CAP, out_width)
        packed = jnp.concatenate([output[:, :, :out_half], output[:, :, out_half:]], axis=1)
        send_out[:, c] = packed.astype(jnp.bfloat16)
        for dst in others():
            if c < RELAY_OUT:

                @pl.when(near_of(dst, pair) != me)
                def _():
                    partial_copy(dst, c).start()
            else:
                out_copy(dst, c, me).start()
        out_copy(partner, c, me).start()
        recv_out[me, c] = send_out[me, c]

    for c in range(RELAY_OUT):
        for dst in others():

            @pl.when(near_of(dst, pair) == me)
            def _():
                partial_copy(dst, c).wait_recv()
                both = send_out[dst, c].astype(jnp.float32) + partial_out[dst, c].astype(
                    jnp.float32
                )
                send_out[dst, c] = both.astype(jnp.bfloat16)
                out_copy(dst, c, 2 * pair).start()

        for k in range(1, flight):
            recv_out[2 * other_pair(k) + 1, c] = jnp.zeros((PACK, out_half), recv_out.dtype)

    for c in list(range(RELAY_OUT, OUT_CHUNKS)) + list(range(RELAY_OUT)):
        lo = c * out_width
        out_copy(partner, c, partner).wait_recv()
        for k in range(1, flight):
            out_copy(partner, c, 2 * other_pair(k)).wait_recv()
            if c >= RELAY_OUT:
                out_copy(partner, c, 2 * other_pair(k) + 1).wait_recv()
        packed = recv_out[:, c].reshape(n * PACK, out_half)
        mixed = jnp.dot(combine, packed, preferred_element_type=jnp.float32).astype(jnp.bfloat16)
        out_ref[:, lo : lo + out_half] = mixed[:tokens]
        out_ref[:, lo + out_half : lo + out_width] = mixed[tokens:]

    for c in range(IN_CHUNKS):
        for dst in row_targets(c):
            row_copy(dst, c).wait_send()
        if c < RELAY_IN:
            for src in others():

                @pl.when(near_of(src, pair) == me)
                def _():
                    relay_copy(src, c).wait_send()

    for c in range(OUT_CHUNKS):
        for dst in others():
            out_copy(dst, c, me).wait_send()
        out_copy(partner, c, me).wait_send()


def body(tokens, expert_ids, gates, weights_in, weights_out):
    n = lax.axis_size("expert")
    flight = n // 2
    local, width = tokens.shape
    hid = weights_out.shape[1]
    in_half = width // IN_CHUNKS // 2
    out_half = width // OUT_CHUNKS // 2
    dtype = tokens.dtype
    return pl.pallas_call(
        partial(kernel, n),
        out_shape=pltpu.VMEM((local, width), dtype),
        in_specs=[pl.BlockSpec(memory_space=pltpu.HBM)] * 5,
        out_specs=pl.BlockSpec(memory_space=pltpu.VMEM),
        scratch_shapes=[
            pltpu.VMEM((local, width), dtype),
            pltpu.VMEM(expert_ids.shape[::-1], expert_ids.dtype),
            pltpu.VMEM(gates.shape[::-1], gates.dtype),
            pltpu.VMEM(weights_in.shape[1:], weights_in.dtype),
            pltpu.VMEM(weights_out.shape[1:], weights_out.dtype),
            pltpu.VMEM((flight, IN_CHUNKS, PACK, in_half), dtype),
            pltpu.VMEM((n, IN_CHUNKS, PACK, in_half), dtype),
            pltpu.VMEM((n, OUT_CHUNKS, PACK, out_half), dtype),
            pltpu.VMEM((n, OUT_CHUNKS, PACK, out_half), dtype),
            pltpu.VMEM((n, max(RELAY_OUT, 1), PACK, out_half), dtype),
            pltpu.SemaphoreType.DMA((3,)),
            pltpu.SemaphoreType.DMA((IN_CHUNKS,)),
            pltpu.SemaphoreType.DMA,
            pltpu.SemaphoreType.DMA((n, IN_CHUNKS)),
            pltpu.SemaphoreType.DMA((n, IN_CHUNKS)),
            pltpu.SemaphoreType.DMA((n, OUT_CHUNKS)),
            pltpu.SemaphoreType.DMA((n, OUT_CHUNKS)),
            pltpu.SemaphoreType.DMA((n, IN_CHUNKS)),
            pltpu.SemaphoreType.DMA((n, OUT_CHUNKS)),
        ],
        compiler_params=pltpu.CompilerParams(
            collective_id=0, has_side_effects=True, vmem_limit_bytes=56 * 2**20
        ),
    )(tokens, expert_ids.T, gates.T, weights_in, weights_out)


def solution(mesh):
    return jax.shard_map(
        body,
        mesh=mesh,
        in_specs=(
            P(("dp", "expert"), None),
            P(("dp", "expert"), None),
            P(("dp", "expert"), None),
            P("expert", None, None),
            P("expert", None, None),
        ),
        out_specs=P(("dp", "expert"), None),
        check_vma=False,
    )
```

```python
from functools import partial

import jax
import jax.numpy as jnp
from jax import lax
from jax.experimental import pallas as pl
from jax.experimental.pallas import tpu as pltpu
from jax.sharding import PartitionSpec as P

SRC_CAP = 8
PACK = 2 * SRC_CAP
IN_CHUNKS = 2
OUT_CHUNKS = 4
RELAY_IN = 1
RELAY_OUT = 0
MESH = pl.DeviceIdType.MESH


def slot_matrix(value, routed, position, rows, rows_per_expert):
    tokens = value[0].shape[1]
    row = lax.broadcasted_iota(jnp.int32, (rows, tokens), 0)
    slot = (row % SRC_CAP).astype(jnp.float32)
    expert = row // rows_per_expert
    table = jnp.zeros((rows, tokens), jnp.float32)
    for e in range(len(value)):
        hit = (expert == e) & (position[e] == slot) & (routed[e] > 0.0)
        table = jnp.where(hit, value[e], table)
    return table


def split_halves(table, axis):
    half = (lax.broadcasted_iota(jnp.int32, table.shape, axis) // SRC_CAP) % 2
    zero = jnp.zeros_like(table)
    return jnp.where(half == 0, table, zero), jnp.where(half == 1, table, zero)


def kernel(
    n,
    tok_hbm,
    ids_hbm,
    gate_hbm,
    win_hbm,
    wout_hbm,
    out_ref,
    tok,
    ids,
    gate,
    win,
    wout,
    send_rows,
    recv_rows,
    send_out,
    recv_out,
    partial_out,
    small_sem,
    win_sem,
    wout_sem,
    row_send_sem,
    row_recv_sem,
    out_send_sem,
    out_recv_sem,
    relay_sem,
    partial_sem,
):
    me = lax.axis_index("expert")
    flight = n // 2
    width = tok.shape[1]
    hid = wout.shape[0]
    in_width = width // IN_CHUNKS
    in_half = in_width // 2
    out_width = width // OUT_CHUNKS
    out_half = out_width // 2

    pair = me // 2
    partner = me + 1 - 2 * (me % 2)

    def peer(d):
        return lax.rem(me + d, n)

    def other_pair(k):
        return lax.rem(pair + k, flight)

    def near_of(source, target_pair):
        return 2 * target_pair + jnp.where(source < 2 * target_pair, 0, 1)

    def others():
        for k in range(1, flight):
            for member in range(2):
                yield 2 * other_pair(k) + member

    barrier = pltpu.get_barrier_semaphore()
    for d in range(1, n):
        pl.semaphore_signal(barrier, inc=1, device_id={"expert": peer(d)}, device_id_type=MESH)

    small = [
        pltpu.make_async_copy(ids_hbm, ids, small_sem.at[0]),
        pltpu.make_async_copy(gate_hbm, gate, small_sem.at[1]),
        pltpu.make_async_copy(tok_hbm, tok, small_sem.at[2]),
    ]
    for copy in small:
        copy.start()

    def win_copy(c):
        rows = pl.ds(c * in_width, in_width)
        return pltpu.make_async_copy(win_hbm.at[0, rows], win.at[rows], win_sem.at[c])

    wout_copy = pltpu.make_async_copy(wout_hbm.at[0], wout, wout_sem)
    for c in range(IN_CHUNKS):
        win_copy(c).start()
    wout_copy.start()

    small[0].wait()
    small[1].wait()
    chosen = ids[...]
    gates = gate[...].astype(jnp.float32)
    tokens = chosen.shape[1]
    weight, routed = [], []
    for e in range(flight):
        match = chosen == e
        weight.append(jnp.sum(jnp.where(match, gates, 0.0), axis=0, keepdims=True))
        routed.append(jnp.sum(jnp.where(match, 1.0, 0.0), axis=0, keepdims=True))
    row = lax.broadcasted_iota(jnp.int32, (PACK, tokens), 0)
    marks = jnp.zeros((PACK, tokens), jnp.float32)
    for e in range(flight):
        marks = jnp.where(row == e, routed[e], marks)
    before = lax.broadcasted_iota(jnp.int32, (tokens, tokens), 0) < lax.broadcasted_iota(
        jnp.int32, (tokens, tokens), 1
    )
    ahead = jnp.dot(
        marks.astype(jnp.bfloat16),
        before.astype(jnp.float32).astype(jnp.bfloat16),
        preferred_element_type=jnp.float32,
    )
    position = [ahead[e : e + 1] for e in range(flight)]
    pick = slot_matrix(routed, routed, position, flight * PACK, PACK)
    pick = [part.astype(jnp.bfloat16) for part in split_halves(pick, 0)]

    def row_copy(dst, c):
        return pltpu.make_async_remote_copy(
            src_ref=send_rows.at[dst // 2, c],
            dst_ref=recv_rows.at[me, c],
            send_sem=row_send_sem.at[dst, c],
            recv_sem=row_recv_sem.at[me, c],
            device_id={"expert": dst},
            device_id_type=MESH,
        )

    def relay_copy(src, c):
        return pltpu.make_async_remote_copy(
            src_ref=recv_rows.at[src, c],
            dst_ref=recv_rows.at[src, c],
            send_sem=relay_sem.at[src, c],
            recv_sem=row_recv_sem.at[src, c],
            device_id={"expert": partner},
            device_id_type=MESH,
        )

    def row_targets(c):
        for k in range(1, flight):
            near = near_of(me, other_pair(k))
            yield near
            if c >= RELAY_IN:
                yield 4 * other_pair(k) + 1 - near
        yield partner

    small[2].wait()
    for c in range(IN_CHUNKS):
        lo = c * in_width
        rows = sum(
            jnp.dot(
                pick[half],
                tok[:, lo + half * in_half : lo + (half + 1) * in_half],
                preferred_element_type=jnp.float32,
            )
            for half in range(2)
        ).astype(jnp.bfloat16)
        send_rows[:, c] = rows.reshape(flight, PACK, in_half)
        if c == 0:
            pl.semaphore_wait(barrier, n - 1)
        for dst in row_targets(c):
            row_copy(dst, c).start()
        recv_rows[me, c] = send_rows[me // 2, c]

    combine = jnp.transpose(slot_matrix(weight, routed, position, n * PACK, 2 * PACK))
    combine = jnp.concatenate(split_halves(combine, 1), axis=0).astype(jnp.bfloat16)

    outer = (me % 2 == 0) == (2 * pair < flight)

    def in_step(step, total):
        c = jnp.where(outer, IN_CHUNKS - 1 - step, step)
        for src in others():
            relay_copy(src, c).wait_recv()

            @pl.when((near_of(src, pair) == me) & (c < RELAY_IN))
            def _():
                relay_copy(src, c).start()

        relay_copy(partner, c).wait_recv()
        win_copy(c).wait()
        packed = recv_rows[:, c].astype(jnp.float32)
        for half in range(2):
            rows = packed[:, half * SRC_CAP : (half + 1) * SRC_CAP].reshape(n * SRC_CAP, in_half)
            start = pl.multiple_of(c * in_width + half * in_half, in_half)
            total = total + jnp.dot(
                rows.astype(jnp.bfloat16),
                win[pl.ds(start, in_half)],
                preferred_element_type=jnp.float32,
            )
        return total

    merged = lax.fori_loop(
        0, IN_CHUNKS, in_step, jnp.zeros((n * SRC_CAP, 2 * hid), jnp.float32)
    )
    left = merged[:, :hid]
    hidden = (left / (1.0 + jnp.exp(-left)) * merged[:, hid:]).astype(jnp.bfloat16)

    def out_copy(dst, c, slot):
        return pltpu.make_async_remote_copy(
            src_ref=send_out.at[dst, c],
            dst_ref=recv_out.at[slot, c],
            send_sem=out_send_sem.at[dst, c],
            recv_sem=out_recv_sem.at[slot, c],
            device_id={"expert": dst},
            device_id_type=MESH,
        )

    def partial_copy(dst, c):
        return pltpu.make_async_remote_copy(
            src_ref=send_out.at[dst, c],
            dst_ref=partial_out.at[dst, c],
            send_sem=out_send_sem.at[dst, c],
            recv_sem=partial_sem.at[dst, c],
            device_id={"expert": partner},
            device_id_type=MESH,
        )

    wout_copy.wait()
    for c in range(OUT_CHUNKS):
        lo = c * out_width
        output = jnp.dot(
            hidden, wout[:, lo : lo + out_width], preferred_element_type=jnp.float32
        ).reshape(n, SRC_CAP, out_width)
        packed = jnp.concatenate([output[:, :, :out_half], output[:, :, out_half:]], axis=1)
        send_out[:, c] = packed.astype(jnp.bfloat16)
        for dst in others():
            if c < RELAY_OUT:

                @pl.when(near_of(dst, pair) != me)
                def _():
                    partial_copy(dst, c).start()
            else:
                out_copy(dst, c, me).start()
        out_copy(partner, c, me).start()
        recv_out[me, c] = send_out[me, c]

    for c in range(RELAY_OUT):
        for dst in others():

            @pl.when(near_of(dst, pair) == me)
            def _():
                partial_copy(dst, c).wait_recv()
                both = send_out[dst, c].astype(jnp.float32) + partial_out[dst, c].astype(
                    jnp.float32
                )
                send_out[dst, c] = both.astype(jnp.bfloat16)
                out_copy(dst, c, 2 * pair).start()

        for k in range(1, flight):
            recv_out[2 * other_pair(k) + 1, c] = jnp.zeros((PACK, out_half), recv_out.dtype)

    for c in list(range(RELAY_OUT, OUT_CHUNKS)) + list(range(RELAY_OUT)):
        lo = c * out_width
        out_copy(partner, c, partner).wait_recv()
        for k in range(1, flight):
            out_copy(partner, c, 2 * other_pair(k)).wait_recv()
            if c >= RELAY_OUT:
                out_copy(partner, c, 2 * other_pair(k) + 1).wait_recv()
        packed = recv_out[:, c].reshape(n * PACK, out_half)
        mixed = jnp.dot(combine, packed, preferred_element_type=jnp.float32).astype(jnp.bfloat16)
        out_ref[:, lo : lo + out_half] = mixed[:tokens]
        out_ref[:, lo + out_half : lo + out_width] = mixed[tokens:]

    for c in range(IN_CHUNKS):
        for dst in row_targets(c):
            row_copy(dst, c).wait_send()
        if c < RELAY_IN:
            for src in others():

                @pl.when(near_of(src, pair) == me)
                def _():
                    relay_copy(src, c).wait_send()

    for c in range(OUT_CHUNKS):
        for dst in others():
            out_copy(dst, c, me).wait_send()
        out_copy(partner, c, me).wait_send()


def body(tokens, expert_ids, gates, weights_in, weights_out):
    n = lax.axis_size("expert")
    flight = n // 2
    local, width = tokens.shape
    hid = weights_out.shape[1]
    in_half = width // IN_CHUNKS // 2
    out_half = width // OUT_CHUNKS // 2
    dtype = tokens.dtype
    return pl.pallas_call(
        partial(kernel, n),
        out_shape=pltpu.VMEM((local, width), dtype),
        in_specs=[pl.BlockSpec(memory_space=pltpu.HBM)] * 5,
        out_specs=pl.BlockSpec(memory_space=pltpu.VMEM),
        scratch_shapes=[
            pltpu.VMEM((local, width), dtype),
            pltpu.VMEM(expert_ids.shape[::-1], expert_ids.dtype),
            pltpu.VMEM(gates.shape[::-1], gates.dtype),
            pltpu.VMEM(weights_in.shape[1:], weights_in.dtype),
            pltpu.VMEM(weights_out.shape[1:], weights_out.dtype),
            pltpu.VMEM((flight, IN_CHUNKS, PACK, in_half), dtype),
            pltpu.VMEM((n, IN_CHUNKS, PACK, in_half), dtype),
            pltpu.VMEM((n, OUT_CHUNKS, PACK, out_half), dtype),
            pltpu.VMEM((n, OUT_CHUNKS, PACK, out_half), dtype),
            pltpu.VMEM((n, max(RELAY_OUT, 1), PACK, out_half), dtype),
            pltpu.SemaphoreType.DMA((3,)),
            pltpu.SemaphoreType.DMA((IN_CHUNKS,)),
            pltpu.SemaphoreType.DMA,
            pltpu.SemaphoreType.DMA((n, IN_CHUNKS)),
            pltpu.SemaphoreType.DMA((n, IN_CHUNKS)),
            pltpu.SemaphoreType.DMA((n, OUT_CHUNKS)),
            pltpu.SemaphoreType.DMA((n, OUT_CHUNKS)),
            pltpu.SemaphoreType.DMA((n, IN_CHUNKS)),
            pltpu.SemaphoreType.DMA((n, OUT_CHUNKS)),
        ],
        compiler_params=pltpu.CompilerParams(
            collective_id=0, has_side_effects=True, vmem_limit_bytes=56 * 2**20
        ),
    )(tokens, expert_ids.T, gates.T, weights_in, weights_out)


def solution(mesh):
    return jax.shard_map(
        body,
        mesh=mesh,
        in_specs=(
            P(("dp", "expert"), None),
            P(("dp", "expert"), None),
            P(("dp", "expert"), None),
            P("expert", None, None),
            P("expert", None, None),
        ),
        out_specs=P(("dp", "expert"), None),
        check_vma=False,
    )
```

```python
from functools import partial

import jax
import jax.numpy as jnp
from jax import lax
from jax.experimental import pallas as pl
from jax.experimental.pallas import tpu as pltpu
from jax.sharding import PartitionSpec as P

SRC_CAP = 8
PACK = 2 * SRC_CAP
IN_CHUNKS = 2
OUT_CHUNKS = 2
RELAY_IN = 1
RELAY_OUT = 0
MESH = pl.DeviceIdType.MESH


def slot_matrix(value, routed, position, rows, rows_per_expert):
    tokens = value[0].shape[1]
    row = lax.broadcasted_iota(jnp.int32, (rows, tokens), 0)
    slot = (row % SRC_CAP).astype(jnp.float32)
    expert = row // rows_per_expert
    table = jnp.zeros((rows, tokens), jnp.float32)
    for e in range(len(value)):
        hit = (expert == e) & (position[e] == slot) & (routed[e] > 0.0)
        table = jnp.where(hit, value[e], table)
    return table


def split_halves(table, axis):
    half = (lax.broadcasted_iota(jnp.int32, table.shape, axis) // SRC_CAP) % 2
    zero = jnp.zeros_like(table)
    return jnp.where(half == 0, table, zero), jnp.where(half == 1, table, zero)


def kernel(
    n,
    tok_hbm,
    ids_hbm,
    gate_hbm,
    win_hbm,
    wout_hbm,
    out_ref,
    tok,
    ids,
    gate,
    win,
    wout,
    send_rows,
    recv_rows,
    send_out,
    recv_out,
    partial_out,
    small_sem,
    win_sem,
    wout_sem,
    row_send_sem,
    row_recv_sem,
    out_send_sem,
    out_recv_sem,
    relay_sem,
    partial_sem,
):
    me = lax.axis_index("expert")
    flight = n // 2
    width = tok.shape[1]
    hid = wout.shape[0]
    in_width = width // IN_CHUNKS
    in_half = in_width // 2
    out_width = width // OUT_CHUNKS
    out_half = out_width // 2

    pair = me // 2
    partner = me + 1 - 2 * (me % 2)

    def peer(d):
        return lax.rem(me + d, n)

    def other_pair(k):
        return lax.rem(pair + k, flight)

    def near_of(source, target_pair):
        return 2 * target_pair + jnp.where(source < 2 * target_pair, 0, 1)

    def others():
        for k in range(1, flight):
            for member in range(2):
                yield 2 * other_pair(k) + member

    barrier = pltpu.get_barrier_semaphore()
    for d in range(1, n):
        pl.semaphore_signal(barrier, inc=1, device_id={"expert": peer(d)}, device_id_type=MESH)

    small = [
        pltpu.make_async_copy(ids_hbm, ids, small_sem.at[0]),
        pltpu.make_async_copy(gate_hbm, gate, small_sem.at[1]),
        pltpu.make_async_copy(tok_hbm, tok, small_sem.at[2]),
    ]
    for copy in small:
        copy.start()

    def win_copy(c):
        rows = pl.ds(pl.multiple_of(c * in_width, in_width), in_width)
        return pltpu.make_async_copy(win_hbm.at[0, rows], win.at[rows], win_sem.at[c])

    wout_copy = pltpu.make_async_copy(wout_hbm.at[0], wout, wout_sem)
    outer = (me % 2 == 0) == (2 * pair < flight)

    def chunk_at(step):
        return jnp.where(outer, IN_CHUNKS - 1 - step, step)

    win_copy(chunk_at(0)).start()

    small[0].wait()
    small[1].wait()
    chosen = ids[...]
    gates = gate[...].astype(jnp.float32)
    tokens = chosen.shape[1]
    weight, routed = [], []
    for e in range(flight):
        match = chosen == e
        weight.append(jnp.sum(jnp.where(match, gates, 0.0), axis=0, keepdims=True))
        routed.append(jnp.sum(jnp.where(match, 1.0, 0.0), axis=0, keepdims=True))
    row = lax.broadcasted_iota(jnp.int32, (PACK, tokens), 0)
    marks = jnp.zeros((PACK, tokens), jnp.float32)
    for e in range(flight):
        marks = jnp.where(row == e, routed[e], marks)
    before = lax.broadcasted_iota(jnp.int32, (tokens, tokens), 0) < lax.broadcasted_iota(
        jnp.int32, (tokens, tokens), 1
    )
    ahead = jnp.dot(
        marks.astype(jnp.bfloat16),
        before.astype(jnp.float32).astype(jnp.bfloat16),
        preferred_element_type=jnp.float32,
    )
    position = [ahead[e : e + 1] for e in range(flight)]
    pick = slot_matrix(routed, routed, position, flight * PACK, PACK)
    pick = [part.astype(jnp.bfloat16) for part in split_halves(pick, 0)]

    def row_copy(dst, c):
        return pltpu.make_async_remote_copy(
            src_ref=send_rows.at[dst // 2, c],
            dst_ref=recv_rows.at[me, c],
            send_sem=row_send_sem.at[dst, c],
            recv_sem=row_recv_sem.at[me, c],
            device_id={"expert": dst},
            device_id_type=MESH,
        )

    def relay_copy(src, c):
        return pltpu.make_async_remote_copy(
            src_ref=recv_rows.at[src, c],
            dst_ref=recv_rows.at[src, c],
            send_sem=relay_sem.at[src, c],
            recv_sem=row_recv_sem.at[src, c],
            device_id={"expert": partner},
            device_id_type=MESH,
        )

    def row_targets(c):
        for k in range(1, flight):
            near = near_of(me, other_pair(k))
            yield near
            if c >= RELAY_IN:
                yield 4 * other_pair(k) + 1 - near
        yield partner

    small[2].wait()
    for c in range(IN_CHUNKS):
        lo = c * in_width
        rows = sum(
            jnp.dot(
                pick[half],
                tok[:, lo + half * in_half : lo + (half + 1) * in_half],
                preferred_element_type=jnp.float32,
            )
            for half in range(2)
        ).astype(jnp.bfloat16)
        send_rows[:, c] = rows.reshape(flight, PACK, in_half)
        if c == 0:
            pl.semaphore_wait(barrier, n - 1)
        for dst in row_targets(c):
            row_copy(dst, c).start()
        recv_rows[me, c] = send_rows[me // 2, c]

    for step in range(1, IN_CHUNKS):
        win_copy(chunk_at(step)).start()
    wout_copy.start()

    combine = jnp.transpose(slot_matrix(weight, routed, position, n * PACK, 2 * PACK))
    combine = jnp.concatenate(split_halves(combine, 1), axis=0).astype(jnp.bfloat16)

    def in_step(step, total):
        c = chunk_at(step)
        for src in others():
            relay_copy(src, c).wait_recv()

            @pl.when((near_of(src, pair) == me) & (c < RELAY_IN))
            def _():
                relay_copy(src, c).start()

        relay_copy(partner, c).wait_recv()
        win_copy(c).wait()
        packed = recv_rows[:, c].astype(jnp.float32)
        for half in range(2):
            rows = packed[:, half * SRC_CAP : (half + 1) * SRC_CAP].reshape(n * SRC_CAP, in_half)
            start = pl.multiple_of(c * in_width + half * in_half, in_half)
            total = total + jnp.dot(
                rows.astype(jnp.bfloat16),
                win[pl.ds(start, in_half)],
                preferred_element_type=jnp.float32,
            )
        return total

    merged = lax.fori_loop(
        0, IN_CHUNKS, in_step, jnp.zeros((n * SRC_CAP, 2 * hid), jnp.float32)
    )
    left = merged[:, :hid]
    hidden = (left / (1.0 + jnp.exp(-left)) * merged[:, hid:]).astype(jnp.bfloat16)

    def out_copy(dst, c, slot):
        return pltpu.make_async_remote_copy(
            src_ref=send_out.at[dst, c],
            dst_ref=recv_out.at[slot, c],
            send_sem=out_send_sem.at[dst, c],
            recv_sem=out_recv_sem.at[slot, c],
            device_id={"expert": dst},
            device_id_type=MESH,
        )

    def partial_copy(dst, c):
        return pltpu.make_async_remote_copy(
            src_ref=send_out.at[dst, c],
            dst_ref=partial_out.at[dst, c],
            send_sem=out_send_sem.at[dst, c],
            recv_sem=partial_sem.at[dst, c],
            device_id={"expert": partner},
            device_id_type=MESH,
        )

    wout_copy.wait()
    for c in range(OUT_CHUNKS):
        lo = c * out_width
        output = jnp.dot(
            hidden, wout[:, lo : lo + out_width], preferred_element_type=jnp.float32
        ).reshape(n, SRC_CAP, out_width)
        packed = jnp.concatenate([output[:, :, :out_half], output[:, :, out_half:]], axis=1)
        send_out[:, c] = packed.astype(jnp.bfloat16)
        for dst in others():
            if c < RELAY_OUT:

                @pl.when(near_of(dst, pair) != me)
                def _():
                    partial_copy(dst, c).start()
            else:
                out_copy(dst, c, me).start()
        out_copy(partner, c, me).start()
        recv_out[me, c] = send_out[me, c]

    for c in range(RELAY_OUT):
        for dst in others():

            @pl.when(near_of(dst, pair) == me)
            def _():
                partial_copy(dst, c).wait_recv()
                both = send_out[dst, c].astype(jnp.float32) + partial_out[dst, c].astype(
                    jnp.float32
                )
                send_out[dst, c] = both.astype(jnp.bfloat16)
                out_copy(dst, c, 2 * pair).start()

        for k in range(1, flight):
            recv_out[2 * other_pair(k) + 1, c] = jnp.zeros((PACK, out_half), recv_out.dtype)

    for c in list(range(RELAY_OUT, OUT_CHUNKS)) + list(range(RELAY_OUT)):
        lo = c * out_width
        out_copy(partner, c, partner).wait_recv()
        for k in range(1, flight):
            out_copy(partner, c, 2 * other_pair(k)).wait_recv()
            if c >= RELAY_OUT:
                out_copy(partner, c, 2 * other_pair(k) + 1).wait_recv()
        packed = recv_out[:, c].reshape(n * PACK, out_half)
        mixed = jnp.dot(combine, packed, preferred_element_type=jnp.float32).astype(jnp.bfloat16)
        out_ref[:, lo : lo + out_half] = mixed[:tokens]
        out_ref[:, lo + out_half : lo + out_width] = mixed[tokens:]

    for c in range(IN_CHUNKS):
        for dst in row_targets(c):
            row_copy(dst, c).wait_send()
        if c < RELAY_IN:
            for src in others():

                @pl.when(near_of(src, pair) == me)
                def _():
                    relay_copy(src, c).wait_send()

    for c in range(OUT_CHUNKS):
        for dst in others():
            out_copy(dst, c, me).wait_send()
        out_copy(partner, c, me).wait_send()


def body(tokens, expert_ids, gates, weights_in, weights_out):
    n = lax.axis_size("expert")
    flight = n // 2
    local, width = tokens.shape
    hid = weights_out.shape[1]
    in_half = width // IN_CHUNKS // 2
    out_half = width // OUT_CHUNKS // 2
    dtype = tokens.dtype
    return pl.pallas_call(
        partial(kernel, n),
        out_shape=pltpu.VMEM((local, width), dtype),
        in_specs=[pl.BlockSpec(memory_space=pltpu.HBM)] * 5,
        out_specs=pl.BlockSpec(memory_space=pltpu.VMEM),
        scratch_shapes=[
            pltpu.VMEM((local, width), dtype),
            pltpu.VMEM(expert_ids.shape[::-1], expert_ids.dtype),
            pltpu.VMEM(gates.shape[::-1], gates.dtype),
            pltpu.VMEM(weights_in.shape[1:], weights_in.dtype),
            pltpu.VMEM(weights_out.shape[1:], weights_out.dtype),
            pltpu.VMEM((flight, IN_CHUNKS, PACK, in_half), dtype),
            pltpu.VMEM((n, IN_CHUNKS, PACK, in_half), dtype),
            pltpu.VMEM((n, OUT_CHUNKS, PACK, out_half), dtype),
            pltpu.VMEM((n, OUT_CHUNKS, PACK, out_half), dtype),
            pltpu.VMEM((n, max(RELAY_OUT, 1), PACK, out_half), dtype),
            pltpu.SemaphoreType.DMA((3,)),
            pltpu.SemaphoreType.DMA((IN_CHUNKS,)),
            pltpu.SemaphoreType.DMA,
            pltpu.SemaphoreType.DMA((n, IN_CHUNKS)),
            pltpu.SemaphoreType.DMA((n, IN_CHUNKS)),
            pltpu.SemaphoreType.DMA((n, OUT_CHUNKS)),
            pltpu.SemaphoreType.DMA((n, OUT_CHUNKS)),
            pltpu.SemaphoreType.DMA((n, IN_CHUNKS)),
            pltpu.SemaphoreType.DMA((n, OUT_CHUNKS)),
        ],
        compiler_params=pltpu.CompilerParams(
            collective_id=0, has_side_effects=True, vmem_limit_bytes=56 * 2**20
        ),
    )(tokens, expert_ids.T, gates.T, weights_in, weights_out)


def solution(mesh):
    return jax.shard_map(
        body,
        mesh=mesh,
        in_specs=(
            P(("dp", "expert"), None),
            P(("dp", "expert"), None),
            P(("dp", "expert"), None),
            P("expert", None, None),
            P("expert", None, None),
        ),
        out_specs=P(("dp", "expert"), None),
        check_vma=False,
    )
```

```python
from functools import partial

import jax
import jax.numpy as jnp
from jax import lax
from jax.experimental import pallas as pl
from jax.experimental.pallas import tpu as pltpu
from jax.sharding import PartitionSpec as P

SRC_CAP = 8
PACK = 2 * SRC_CAP
IN_CHUNKS = 2
OUT_CHUNKS = 2
RELAY_IN = 1
RELAY_OUT = 1
MESH = pl.DeviceIdType.MESH


def slot_matrix(value, routed, position, rows, rows_per_expert):
    tokens = value[0].shape[1]
    row = lax.broadcasted_iota(jnp.int32, (rows, tokens), 0)
    slot = (row % SRC_CAP).astype(jnp.float32)
    expert = row // rows_per_expert
    table = jnp.zeros((rows, tokens), jnp.float32)
    for e in range(len(value)):
        hit = (expert == e) & (position[e] == slot) & (routed[e] > 0.0)
        table = jnp.where(hit, value[e], table)
    return table


def split_halves(table, axis):
    half = (lax.broadcasted_iota(jnp.int32, table.shape, axis) // SRC_CAP) % 2
    zero = jnp.zeros_like(table)
    return jnp.where(half == 0, table, zero), jnp.where(half == 1, table, zero)


def kernel(
    n,
    tok_hbm,
    ids_hbm,
    gate_hbm,
    win_hbm,
    wout_hbm,
    out_ref,
    tok,
    ids,
    gate,
    win,
    wout,
    send_rows,
    recv_rows,
    send_out,
    recv_out,
    partial_out,
    small_sem,
    win_sem,
    wout_sem,
    row_send_sem,
    row_recv_sem,
    out_send_sem,
    out_recv_sem,
    relay_sem,
    partial_sem,
):
    me = lax.axis_index("expert")
    flight = n // 2
    width = tok.shape[1]
    hid = wout.shape[0]
    in_width = width // IN_CHUNKS
    in_half = in_width // 2
    out_width = width // OUT_CHUNKS
    out_half = out_width // 2

    lean = lax.axis_index("dp") % 2 == 1
    pair = me // 2
    partner = me + 1 - 2 * (me % 2)

    def peer(d):
        return lax.rem(me + d, n)

    def other_pair(k):
        return lax.rem(pair + k, flight)

    def near_of(source, target_pair):
        return 2 * target_pair + jnp.where(source < 2 * target_pair, 0, 1)

    def others():
        for k in range(1, flight):
            for member in range(2):
                yield 2 * other_pair(k) + member

    barrier = pltpu.get_barrier_semaphore()
    for d in range(1, n):
        pl.semaphore_signal(barrier, inc=1, device_id={"expert": peer(d)}, device_id_type=MESH)

    small = [
        pltpu.make_async_copy(ids_hbm, ids, small_sem.at[0]),
        pltpu.make_async_copy(gate_hbm, gate, small_sem.at[1]),
        pltpu.make_async_copy(tok_hbm, tok, small_sem.at[2]),
    ]
    for copy in small:
        copy.start()

    def win_copy(c):
        rows = pl.ds(c * in_width, in_width)
        return pltpu.make_async_copy(win_hbm.at[0, rows], win.at[rows], win_sem.at[c])

    wout_copy = pltpu.make_async_copy(wout_hbm.at[0], wout, wout_sem)
    for c in range(IN_CHUNKS):
        win_copy(c).start()
    wout_copy.start()

    small[0].wait()
    small[1].wait()
    chosen = ids[...]
    gates = gate[...].astype(jnp.float32)
    tokens = chosen.shape[1]
    weight, routed = [], []
    for e in range(flight):
        match = chosen == e
        weight.append(jnp.sum(jnp.where(match, gates, 0.0), axis=0, keepdims=True))
        routed.append(jnp.sum(jnp.where(match, 1.0, 0.0), axis=0, keepdims=True))
    row = lax.broadcasted_iota(jnp.int32, (PACK, tokens), 0)
    marks = jnp.zeros((PACK, tokens), jnp.float32)
    for e in range(flight):
        marks = jnp.where(row == e, routed[e], marks)
    before = lax.broadcasted_iota(jnp.int32, (tokens, tokens), 0) < lax.broadcasted_iota(
        jnp.int32, (tokens, tokens), 1
    )
    ahead = jnp.dot(
        marks.astype(jnp.bfloat16),
        before.astype(jnp.float32).astype(jnp.bfloat16),
        preferred_element_type=jnp.float32,
    )
    position = [ahead[e : e + 1] for e in range(flight)]
    pick = slot_matrix(routed, routed, position, flight * PACK, PACK)
    pick = [part.astype(jnp.bfloat16) for part in split_halves(pick, 0)]

    def row_copy(dst, c):
        return pltpu.make_async_remote_copy(
            src_ref=send_rows.at[dst // 2, c],
            dst_ref=recv_rows.at[me, c],
            send_sem=row_send_sem.at[dst, c],
            recv_sem=row_recv_sem.at[me, c],
            device_id={"expert": dst},
            device_id_type=MESH,
        )

    def relay_copy(src, c):
        return pltpu.make_async_remote_copy(
            src_ref=recv_rows.at[src, c],
            dst_ref=recv_rows.at[src, c],
            send_sem=relay_sem.at[src, c],
            recv_sem=row_recv_sem.at[src, c],
            device_id={"expert": partner},
            device_id_type=MESH,
        )

    def for_row_targets(c, act):
        for k in range(1, flight):
            near = near_of(me, other_pair(k))
            act(row_copy(near, c))
            if c >= RELAY_IN:

                @pl.when(jnp.logical_not(lean))
                def _():
                    act(row_copy(4 * other_pair(k) + 1 - near, c))

        act(row_copy(partner, c))

    small[2].wait()
    for c in range(IN_CHUNKS):
        lo = c * in_width
        rows = sum(
            jnp.dot(
                pick[half],
                tok[:, lo + half * in_half : lo + (half + 1) * in_half],
                preferred_element_type=jnp.float32,
            )
            for half in range(2)
        ).astype(jnp.bfloat16)
        send_rows[:, c] = rows.reshape(flight, PACK, in_half)
        if c == 0:
            pl.semaphore_wait(barrier, n - 1)
        for_row_targets(c, lambda copy: copy.start())
        recv_rows[me, c] = send_rows[me // 2, c]

    combine = jnp.transpose(slot_matrix(weight, routed, position, n * PACK, 2 * PACK))
    combine = jnp.concatenate(split_halves(combine, 1), axis=0).astype(jnp.bfloat16)

    outer = ((me % 2 == 0) == (2 * pair < flight)) & jnp.logical_not(lean)

    def in_step(step, total):
        c = jnp.where(outer, IN_CHUNKS - 1 - step, step)
        for src in others():
            relay_copy(src, c).wait_recv()

            @pl.when((near_of(src, pair) == me) & (lean | (c < RELAY_IN)))
            def _():
                relay_copy(src, c).start()

        relay_copy(partner, c).wait_recv()
        win_copy(c).wait()
        packed = recv_rows[:, c].astype(jnp.float32)
        for half in range(2):
            rows = packed[:, half * SRC_CAP : (half + 1) * SRC_CAP].reshape(n * SRC_CAP, in_half)
            start = pl.multiple_of(c * in_width + half * in_half, in_half)
            total = total + jnp.dot(
                rows.astype(jnp.bfloat16),
                win[pl.ds(start, in_half)],
                preferred_element_type=jnp.float32,
            )
        return total

    merged = lax.fori_loop(
        0, IN_CHUNKS, in_step, jnp.zeros((n * SRC_CAP, 2 * hid), jnp.float32)
    )
    left = merged[:, :hid]
    hidden = (left / (1.0 + jnp.exp(-left)) * merged[:, hid:]).astype(jnp.bfloat16)

    def out_copy(dst, c, slot):
        return pltpu.make_async_remote_copy(
            src_ref=send_out.at[dst, c],
            dst_ref=recv_out.at[slot, c],
            send_sem=out_send_sem.at[dst, c],
            recv_sem=out_recv_sem.at[slot, c],
            device_id={"expert": dst},
            device_id_type=MESH,
        )

    def partial_copy(dst, c):
        return pltpu.make_async_remote_copy(
            src_ref=send_out.at[dst, c],
            dst_ref=partial_out.at[dst, c],
            send_sem=out_send_sem.at[dst, c],
            recv_sem=partial_sem.at[dst, c],
            device_id={"expert": partner},
            device_id_type=MESH,
        )

    wout_copy.wait()
    for c in range(OUT_CHUNKS):
        lo = c * out_width
        output = jnp.dot(
            hidden, wout[:, lo : lo + out_width], preferred_element_type=jnp.float32
        ).reshape(n, SRC_CAP, out_width)
        packed = jnp.concatenate([output[:, :, :out_half], output[:, :, out_half:]], axis=1)
        send_out[:, c] = packed.astype(jnp.bfloat16)
        for dst in others():
            if c < RELAY_OUT:

                @pl.when(lean & (near_of(dst, pair) != me))
                def _():
                    partial_copy(dst, c).start()

                @pl.when(jnp.logical_not(lean))
                def _():
                    out_copy(dst, c, me).start()
            else:
                out_copy(dst, c, me).start()
        out_copy(partner, c, me).start()
        recv_out[me, c] = send_out[me, c]

    for c in range(RELAY_OUT):
        for dst in others():

            @pl.when(lean & (near_of(dst, pair) == me))
            def _():
                partial_copy(dst, c).wait_recv()
                both = send_out[dst, c].astype(jnp.float32) + partial_out[dst, c].astype(
                    jnp.float32
                )
                send_out[dst, c] = both.astype(jnp.bfloat16)
                out_copy(dst, c, 2 * pair).start()

        for k in range(1, flight):

            @pl.when(lean)
            def _():
                recv_out[2 * other_pair(k) + 1, c] = jnp.zeros((PACK, out_half), recv_out.dtype)

    for step in range(OUT_CHUNKS):
        c = jnp.where(lean, OUT_CHUNKS - 1 - step, step)
        out_copy(partner, c, partner).wait_recv()
        for k in range(1, flight):
            out_copy(partner, c, 2 * other_pair(k)).wait_recv()

            @pl.when(jnp.logical_not(lean) | (c >= RELAY_OUT))
            def _():
                out_copy(partner, c, 2 * other_pair(k) + 1).wait_recv()

        packed = recv_out[:, c].reshape(n * PACK, out_half)
        mixed = jnp.dot(combine, packed, preferred_element_type=jnp.float32).astype(jnp.bfloat16)
        for half in range(2):
            lo = pl.multiple_of(c * out_width + half * out_half, out_half)
            out_ref[:, pl.ds(lo, out_half)] = mixed[half * tokens : (half + 1) * tokens]

    for c in range(IN_CHUNKS):
        for_row_targets(c, lambda copy: copy.wait_send())
        for src in others():

            @pl.when((near_of(src, pair) == me) & (lean | (c < RELAY_IN)))
            def _():
                relay_copy(src, c).wait_send()

    for c in range(OUT_CHUNKS):
        for dst in others():
            out_copy(dst, c, me).wait_send()
        out_copy(partner, c, me).wait_send()


def body(tokens, expert_ids, gates, weights_in, weights_out):
    n = lax.axis_size("expert")
    flight = n // 2
    local, width = tokens.shape
    hid = weights_out.shape[1]
    in_half = width // IN_CHUNKS // 2
    out_half = width // OUT_CHUNKS // 2
    dtype = tokens.dtype
    return pl.pallas_call(
        partial(kernel, n),
        out_shape=pltpu.VMEM((local, width), dtype),
        in_specs=[pl.BlockSpec(memory_space=pltpu.HBM)] * 5,
        out_specs=pl.BlockSpec(memory_space=pltpu.VMEM),
        scratch_shapes=[
            pltpu.VMEM((local, width), dtype),
            pltpu.VMEM(expert_ids.shape[::-1], expert_ids.dtype),
            pltpu.VMEM(gates.shape[::-1], gates.dtype),
            pltpu.VMEM(weights_in.shape[1:], weights_in.dtype),
            pltpu.VMEM(weights_out.shape[1:], weights_out.dtype),
            pltpu.VMEM((flight, IN_CHUNKS, PACK, in_half), dtype),
            pltpu.VMEM((n, IN_CHUNKS, PACK, in_half), dtype),
            pltpu.VMEM((n, OUT_CHUNKS, PACK, out_half), dtype),
            pltpu.VMEM((n, OUT_CHUNKS, PACK, out_half), dtype),
            pltpu.VMEM((n, max(RELAY_OUT, 1), PACK, out_half), dtype),
            pltpu.SemaphoreType.DMA((3,)),
            pltpu.SemaphoreType.DMA((IN_CHUNKS,)),
            pltpu.SemaphoreType.DMA,
            pltpu.SemaphoreType.DMA((n, IN_CHUNKS)),
            pltpu.SemaphoreType.DMA((n, IN_CHUNKS)),
            pltpu.SemaphoreType.DMA((n, OUT_CHUNKS)),
            pltpu.SemaphoreType.DMA((n, OUT_CHUNKS)),
            pltpu.SemaphoreType.DMA((n, IN_CHUNKS)),
            pltpu.SemaphoreType.DMA((n, OUT_CHUNKS)),
        ],
        compiler_params=pltpu.CompilerParams(
            collective_id=0, has_side_effects=True, vmem_limit_bytes=56 * 2**20
        ),
    )(tokens, expert_ids.T, gates.T, weights_in, weights_out)


def solution(mesh):
    return jax.shard_map(
        body,
        mesh=mesh,
        in_specs=(
            P(("dp", "expert"), None),
            P(("dp", "expert"), None),
            P(("dp", "expert"), None),
            P("expert", None, None),
            P("expert", None, None),
        ),
        out_specs=P(("dp", "expert"), None),
        check_vma=False,
    )
```

```python
from functools import partial

import jax
import jax.numpy as jnp
from jax import lax
from jax.experimental import pallas as pl
from jax.experimental.pallas import tpu as pltpu
from jax.sharding import PartitionSpec as P

SRC_CAP = 8
PACK = 2 * SRC_CAP
IN_CHUNKS = 2
OUT_CHUNKS = 2
RELAY_IN = 1
MESH = pl.DeviceIdType.MESH


def slot_matrix(value, routed, position, rows, rows_per_expert):
    tokens = value[0].shape[1]
    row = lax.broadcasted_iota(jnp.int32, (rows, tokens), 0)
    slot = (row % SRC_CAP).astype(jnp.float32)
    expert = row // rows_per_expert
    table = jnp.zeros((rows, tokens), jnp.float32)
    for e in range(len(value)):
        hit = (expert == e) & (position[e] == slot) & (routed[e] > 0.0)
        table = jnp.where(hit, value[e], table)
    return table


def split_halves(table, axis):
    half = (lax.broadcasted_iota(jnp.int32, table.shape, axis) // SRC_CAP) % 2
    zero = jnp.zeros_like(table)
    return jnp.where(half == 0, table, zero), jnp.where(half == 1, table, zero)


def kernel(
    n,
    tok_hbm,
    ids_hbm,
    gate_hbm,
    win_hbm,
    wout_hbm,
    out_ref,
    tok,
    ids,
    gate,
    win,
    wout,
    send_rows,
    recv_rows,
    send_out,
    recv_out,
    small_sem,
    win_sem,
    wout_sem,
    row_send_sem,
    row_recv_sem,
    out_send_sem,
    out_recv_sem,
    relay_sem,
):
    me = lax.axis_index("expert")
    flight = n // 2
    width = tok.shape[1]
    hid = wout.shape[0]
    in_width = width // IN_CHUNKS
    in_half = in_width // 2
    out_width = width // OUT_CHUNKS
    out_half = out_width // 2

    pair = me // 2
    partner = me + 1 - 2 * (me % 2)

    def wrapped(index, count):
        return jnp.where(index >= count, index - count, index)

    peers = [wrapped(me + d, n) for d in range(1, n)]
    other_pairs = [wrapped(pair + k, flight) for k in range(1, flight)]
    others = [2 * other + member for other in other_pairs for member in range(2)]
    nears = [2 * other + jnp.where(me < 2 * other, 0, 1) for other in other_pairs]
    fars = [4 * other + 1 - near for other, near in zip(other_pairs, nears)]
    near_to = [(other < pair) == (me == 2 * pair) for other in other_pairs for _ in range(2)]

    small = [
        pltpu.make_async_copy(ids_hbm, ids, small_sem.at[0]),
        pltpu.make_async_copy(gate_hbm, gate, small_sem.at[1]),
        pltpu.make_async_copy(tok_hbm, tok, small_sem.at[2]),
    ]
    for copy in small:
        copy.start()

    barrier = pltpu.get_barrier_semaphore()
    for peer in peers:
        pl.semaphore_signal(barrier, inc=1, device_id={"expert": peer}, device_id_type=MESH)

    def win_copy(c):
        rows = pl.ds(c * in_width, in_width)
        return pltpu.make_async_copy(win_hbm.at[0, rows], win.at[rows], win_sem.at[c])

    wout_copy = pltpu.make_async_copy(wout_hbm.at[0], wout, wout_sem)
    for c in range(IN_CHUNKS):
        win_copy(c).start()
    wout_copy.start()

    small[0].wait()
    small[1].wait()
    chosen = ids[...]
    gates = gate[...].astype(jnp.float32)
    tokens = chosen.shape[1]
    weight, routed = [], []
    for e in range(flight):
        match = chosen == e
        weight.append(jnp.sum(jnp.where(match, gates, 0.0), axis=0, keepdims=True))
        routed.append(jnp.sum(jnp.where(match, 1.0, 0.0), axis=0, keepdims=True))
    row = lax.broadcasted_iota(jnp.int32, (PACK, tokens), 0)
    marks = jnp.zeros((PACK, tokens), jnp.float32)
    for e in range(flight):
        marks = jnp.where(row == e, routed[e], marks)
    before = lax.broadcasted_iota(jnp.int32, (tokens, tokens), 0) < lax.broadcasted_iota(
        jnp.int32, (tokens, tokens), 1
    )
    ahead = jnp.dot(
        marks.astype(jnp.bfloat16),
        before.astype(jnp.float32).astype(jnp.bfloat16),
        preferred_element_type=jnp.float32,
    )
    position = [ahead[e : e + 1] for e in range(flight)]
    pick = slot_matrix(routed, routed, position, flight * PACK, PACK)
    pick = [part.astype(jnp.bfloat16) for part in split_halves(pick, 0)]

    def row_copy(dst, c):
        return pltpu.make_async_remote_copy(
            src_ref=send_rows.at[dst // 2, c],
            dst_ref=recv_rows.at[me, c],
            send_sem=row_send_sem.at[dst, c],
            recv_sem=row_recv_sem.at[me, c],
            device_id={"expert": dst},
            device_id_type=MESH,
        )

    def relay_copy(src, c):
        return pltpu.make_async_remote_copy(
            src_ref=recv_rows.at[src, c],
            dst_ref=recv_rows.at[src, c],
            send_sem=relay_sem.at[src, c],
            recv_sem=row_recv_sem.at[src, c],
            device_id={"expert": partner},
            device_id_type=MESH,
        )

    def row_targets(c):
        return nears + (fars if c >= RELAY_IN else []) + [partner]

    small[2].wait()
    for c in range(IN_CHUNKS):
        lo = c * in_width
        rows = sum(
            jnp.dot(
                pick[half],
                tok[:, lo + half * in_half : lo + (half + 1) * in_half],
                preferred_element_type=jnp.float32,
            )
            for half in range(2)
        ).astype(jnp.bfloat16)
        send_rows[:, c] = rows.reshape(flight, PACK, in_half)
        if c == 0:
            pl.semaphore_wait(barrier, n - 1)
        for dst in row_targets(c):
            row_copy(dst, c).start()
        recv_rows[me, c] = send_rows[me // 2, c]

    combine = jnp.transpose(slot_matrix(weight, routed, position, n * PACK, 2 * PACK))
    combine = jnp.concatenate(split_halves(combine, 1), axis=0).astype(jnp.bfloat16)

    outer = (me % 2 == 0) == (2 * pair < flight)

    merged = jnp.zeros((n * SRC_CAP, 2 * hid), jnp.float32)
    for step in range(IN_CHUNKS):
        c = jnp.where(outer, IN_CHUNKS - 1 - step, step)
        for src, near in zip(others, near_to):
            relay_copy(src, c).wait_recv()

            @pl.when(near & (c < RELAY_IN))
            def _():
                relay_copy(src, c).start()

        relay_copy(partner, c).wait_recv()
        win_copy(c).wait()
        packed = recv_rows[:, c].astype(jnp.float32)
        for half in range(2):
            rows = packed[:, half * SRC_CAP : (half + 1) * SRC_CAP].reshape(n * SRC_CAP, in_half)
            start = pl.multiple_of(c * in_width + half * in_half, in_half)
            merged = merged + jnp.dot(
                rows.astype(jnp.bfloat16),
                win[pl.ds(start, in_half)],
                preferred_element_type=jnp.float32,
            )

    left = merged[:, :hid]
    hidden = (left / (1.0 + jnp.exp(-left)) * merged[:, hid:]).astype(jnp.bfloat16)

    def out_copy(dst, c, slot):
        return pltpu.make_async_remote_copy(
            src_ref=send_out.at[dst, c],
            dst_ref=recv_out.at[slot, c],
            send_sem=out_send_sem.at[dst, c],
            recv_sem=out_recv_sem.at[slot, c],
            device_id={"expert": dst},
            device_id_type=MESH,
        )

    wout_copy.wait()
    for c in range(OUT_CHUNKS):
        lo = c * out_width
        output = jnp.dot(
            hidden, wout[:, lo : lo + out_width], preferred_element_type=jnp.float32
        ).reshape(n, SRC_CAP, out_width)
        packed = jnp.concatenate([output[:, :, :out_half], output[:, :, out_half:]], axis=1)
        send_out[:, c] = packed.astype(jnp.bfloat16)
        for dst in others:
            out_copy(dst, c, me).start()
        out_copy(partner, c, me).start()
        recv_out[me, c] = send_out[me, c]

    for c in range(IN_CHUNKS):
        for dst in row_targets(c):
            row_copy(dst, c).wait_send()
        if c < RELAY_IN:
            for src, near in zip(others, near_to):

                @pl.when(near)
                def _():
                    relay_copy(src, c).wait_send()

    for c in range(OUT_CHUNKS):
        lo = c * out_width
        for peer in others + [partner]:
            out_copy(peer, c, me).wait_send()
        for peer in others + [partner]:
            out_copy(partner, c, peer).wait_recv()
        packed = recv_out[:, c].reshape(n * PACK, out_half)
        mixed = jnp.dot(combine, packed, preferred_element_type=jnp.float32).astype(jnp.bfloat16)
        out_ref[:, lo : lo + out_half] = mixed[:tokens]
        out_ref[:, lo + out_half : lo + out_width] = mixed[tokens:]


def body(tokens, expert_ids, gates, weights_in, weights_out):
    n = lax.axis_size("expert")
    flight = n // 2
    local, width = tokens.shape
    hid = weights_out.shape[1]
    in_half = width // IN_CHUNKS // 2
    out_half = width // OUT_CHUNKS // 2
    dtype = tokens.dtype
    return pl.pallas_call(
        partial(kernel, n),
        out_shape=pltpu.VMEM((local, width), dtype),
        in_specs=[pl.BlockSpec(memory_space=pltpu.HBM)] * 5,
        out_specs=pl.BlockSpec(memory_space=pltpu.VMEM),
        scratch_shapes=[
            pltpu.VMEM((local, width), dtype),
            pltpu.VMEM(expert_ids.shape[::-1], expert_ids.dtype),
            pltpu.VMEM(gates.shape[::-1], gates.dtype),
            pltpu.VMEM(weights_in.shape[1:], weights_in.dtype),
            pltpu.VMEM(weights_out.shape[1:], weights_out.dtype),
            pltpu.VMEM((flight, IN_CHUNKS, PACK, in_half), dtype),
            pltpu.VMEM((n, IN_CHUNKS, PACK, in_half), dtype),
            pltpu.VMEM((n, OUT_CHUNKS, PACK, out_half), dtype),
            pltpu.VMEM((n, OUT_CHUNKS, PACK, out_half), dtype),
            pltpu.SemaphoreType.DMA((3,)),
            pltpu.SemaphoreType.DMA((IN_CHUNKS,)),
            pltpu.SemaphoreType.DMA,
            pltpu.SemaphoreType.DMA((n, IN_CHUNKS)),
            pltpu.SemaphoreType.DMA((n, IN_CHUNKS)),
            pltpu.SemaphoreType.DMA((n, OUT_CHUNKS)),
            pltpu.SemaphoreType.DMA((n, OUT_CHUNKS)),
            pltpu.SemaphoreType.DMA((n, IN_CHUNKS)),
        ],
        compiler_params=pltpu.CompilerParams(
            collective_id=0, has_side_effects=True, vmem_limit_bytes=56 * 2**20
        ),
    )(tokens, expert_ids.T, gates.T, weights_in, weights_out)


def solution(mesh):
    return jax.shard_map(
        body,
        mesh=mesh,
        in_specs=(
            P(("dp", "expert"), None),
            P(("dp", "expert"), None),
            P(("dp", "expert"), None),
            P("expert", None, None),
            P("expert", None, None),
        ),
        out_specs=P(("dp", "expert"), None),
        check_vma=False,
    )
```

```python
from functools import partial

import jax
import jax.numpy as jnp
from jax import lax
from jax.experimental import pallas as pl
from jax.experimental.pallas import tpu as pltpu
from jax.sharding import PartitionSpec as P

SRC_CAP = 8
PACK = 2 * SRC_CAP
GROUPS = 2
SLOTS = SRC_CAP // GROUPS
PARTS = PACK // SLOTS
RELAY = 1
MESH = pl.DeviceIdType.MESH


def slot_matrix(value, routed, position, rows, rows_per_expert, group):
    tokens = value[0].shape[1]
    row = lax.broadcasted_iota(jnp.int32, (rows, tokens), 0)
    slot = (row % SLOTS + group * SLOTS).astype(jnp.float32)
    expert = row // rows_per_expert
    table = jnp.zeros((rows, tokens), jnp.float32)
    for e in range(len(value)):
        hit = (expert == e) & (position[e] == slot) & (routed[e] > 0.0)
        table = jnp.where(hit, value[e], table)
    return table


def split_parts(table, axis):
    part = (lax.broadcasted_iota(jnp.int32, table.shape, axis) // SLOTS) % PARTS
    return [jnp.where(part == p, table, jnp.zeros_like(table)) for p in range(PARTS)]


def kernel(
    n,
    tok_hbm,
    ids_hbm,
    gate_hbm,
    win_hbm,
    wout_hbm,
    out_ref,
    tok,
    ids,
    gate,
    win,
    wout,
    send_rows,
    recv_rows,
    send_out,
    recv_out,
    small_sem,
    win_sem,
    wout_sem,
    row_send_sem,
    row_recv_sem,
    out_send_sem,
    out_recv_sem,
    relay_sem,
):
    me = lax.axis_index("expert")
    flight = n // 2
    width = tok.shape[1]
    hid = wout.shape[0]
    part_width = width // PARTS
    half_width = width // 2
    pair = me // 2
    partner = me + 1 - 2 * (me % 2)

    def wrapped(index, count):
        return jnp.where(index >= count, index - count, index)

    peers = [wrapped(me + d, n) for d in range(1, n)]
    other_pairs = [wrapped(pair + k, flight) for k in range(1, flight)]
    others = [2 * other + member for other in other_pairs for member in range(2)]
    nears = [2 * other + jnp.where(me < 2 * other, 0, 1) for other in other_pairs]
    fars = [4 * other + 1 - near for other, near in zip(other_pairs, nears)]
    near_to = [(other < pair) == (me == 2 * pair) for other in other_pairs for _ in range(2)]

    small = [
        pltpu.make_async_copy(ids_hbm, ids, small_sem.at[0]),
        pltpu.make_async_copy(gate_hbm, gate, small_sem.at[1]),
        pltpu.make_async_copy(tok_hbm, tok, small_sem.at[2]),
    ]
    for copy in small:
        copy.start()

    barrier = pltpu.get_barrier_semaphore()
    for peer in peers:
        pl.semaphore_signal(barrier, inc=1, device_id={"expert": peer}, device_id_type=MESH)

    def win_copy(c):
        rows = pl.ds(c * half_width, half_width)
        return pltpu.make_async_copy(win_hbm.at[0, rows], win.at[rows], win_sem.at[c])

    wout_copy = pltpu.make_async_copy(wout_hbm.at[0], wout, wout_sem)
    for c in range(2):
        win_copy(c).start()
    wout_copy.start()

    small[0].wait()
    small[1].wait()
    chosen = ids[...]
    gates = gate[...].astype(jnp.float32)
    tokens = chosen.shape[1]
    weight, routed = [], []
    for e in range(flight):
        match = chosen == e
        weight.append(jnp.sum(jnp.where(match, gates, 0.0), axis=0, keepdims=True))
        routed.append(jnp.sum(jnp.where(match, 1.0, 0.0), axis=0, keepdims=True))
    row = lax.broadcasted_iota(jnp.int32, (PACK, tokens), 0)
    marks = jnp.zeros((PACK, tokens), jnp.float32)
    for e in range(flight):
        marks = jnp.where(row == e, routed[e], marks)
    before = lax.broadcasted_iota(jnp.int32, (tokens, tokens), 0) < lax.broadcasted_iota(
        jnp.int32, (tokens, tokens), 1
    )
    ahead = jnp.dot(
        marks.astype(jnp.bfloat16),
        before.astype(jnp.float32).astype(jnp.bfloat16),
        preferred_element_type=jnp.float32,
    )
    position = [ahead[e : e + 1] for e in range(flight)]
    pick = [
        [
            part.astype(jnp.bfloat16)
            for part in split_parts(
                slot_matrix(routed, routed, position, flight * PACK, PACK, g), 0
            )
        ]
        for g in range(GROUPS)
    ]

    def row_copy(dst, c):
        return pltpu.make_async_remote_copy(
            src_ref=send_rows.at[dst // 2, c],
            dst_ref=recv_rows.at[me, c],
            send_sem=row_send_sem.at[dst, c],
            recv_sem=row_recv_sem.at[me, c],
            device_id={"expert": dst},
            device_id_type=MESH,
        )

    def relay_copy(src, c):
        return pltpu.make_async_remote_copy(
            src_ref=recv_rows.at[src, c],
            dst_ref=recv_rows.at[src, c],
            send_sem=relay_sem.at[src, c],
            recv_sem=row_recv_sem.at[src, c],
            device_id={"expert": partner},
            device_id_type=MESH,
        )

    def row_targets(c):
        return nears + (fars if c >= RELAY else []) + [partner]

    small[2].wait()
    for c in range(GROUPS):
        rows = sum(
            jnp.dot(
                pick[c][p],
                tok[:, p * part_width : (p + 1) * part_width],
                preferred_element_type=jnp.float32,
            )
            for p in range(PARTS)
        ).astype(jnp.bfloat16)
        send_rows[:, c] = rows.reshape(flight, PACK, part_width)
        if c == 0:
            pl.semaphore_wait(barrier, n - 1)
        for dst in row_targets(c):
            row_copy(dst, c).start()
        recv_rows[me, c] = send_rows[me // 2, c]

    combine = []
    for g in range(GROUPS):
        table = slot_matrix(weight, routed, position, n * PACK, 2 * PACK, g)
        combine.append(jnp.concatenate(split_parts(jnp.transpose(table), 1), axis=0))
    combine = [table.astype(jnp.bfloat16) for table in combine]

    outer = (me % 2 == 0) == (2 * pair < flight)

    def out_copy(dst, c, slot):
        return pltpu.make_async_remote_copy(
            src_ref=send_out.at[dst, c],
            dst_ref=recv_out.at[slot, c],
            send_sem=out_send_sem.at[dst, c],
            recv_sem=out_recv_sem.at[slot, c],
            device_id={"expert": dst},
            device_id_type=MESH,
        )

    for step in range(GROUPS):
        c = jnp.where(outer, GROUPS - 1 - step, step)
        for src, near in zip(others, near_to):
            relay_copy(src, c).wait_recv()

            @pl.when(near & (c < RELAY))
            def _():
                relay_copy(src, c).start()

        relay_copy(partner, c).wait_recv()
        if step == 0:
            win_copy(0).wait()
            win_copy(1).wait()
        packed = recv_rows[:, c].reshape(n * PACK, part_width).astype(jnp.float32)
        merged = jnp.zeros((n * PACK, 2 * hid), jnp.float32)
        for p, rows in enumerate(split_parts(packed, 0)):
            merged = merged + jnp.dot(
                rows.astype(jnp.bfloat16),
                win[p * part_width : (p + 1) * part_width],
                preferred_element_type=jnp.float32,
            )
        merged = merged.reshape(n, PACK, 2 * hid)
        merged = (merged[:, :SRC_CAP] + merged[:, SRC_CAP:]).reshape(n * SRC_CAP, 2 * hid)
        swapped = merged.reshape(n, SRC_CAP, 2 * hid)
        swapped = pltpu.roll(swapped, SLOTS, 1).reshape(n * SRC_CAP, 2 * hid)
        merged = merged + swapped
        left = merged[:, :hid]
        hidden = (left / (1.0 + jnp.exp(-left)) * merged[:, hid:]).astype(jnp.bfloat16)

        if step == 0:
            wout_copy.wait()
        first = lax.broadcasted_iota(jnp.int32, (n, SRC_CAP, part_width), 1) < SLOTS
        for half in range(2):
            output = [
                jnp.dot(
                    hidden,
                    wout[:, p * part_width : (p + 1) * part_width],
                    preferred_element_type=jnp.float32,
                ).reshape(n, SRC_CAP, part_width)
                for p in (2 * half, 2 * half + 1)
            ]
            if half == 0:
                lower = jnp.where(first, output[0], output[1])
            else:
                upper = jnp.where(first, output[0], output[1])
        send_out[:, c] = jnp.concatenate([lower, upper], axis=1).astype(jnp.bfloat16)
        for peer in others + [partner]:
            out_copy(peer, c, me).start()
        recv_out[me, c] = send_out[me, c]

    for c in range(GROUPS):
        for dst in row_targets(c):
            row_copy(dst, c).wait_send()
        if c < RELAY:
            for src, near in zip(others, near_to):

                @pl.when(near)
                def _():
                    relay_copy(src, c).wait_send()

    for c in range(GROUPS):
        for peer in others + [partner]:
            out_copy(peer, c, me).wait_send()
        for peer in others + [partner]:
            out_copy(partner, c, peer).wait_recv()
    mixed = sum(
        jnp.dot(
            combine[g],
            recv_out[:, g].reshape(n * PACK, part_width),
            preferred_element_type=jnp.float32,
        )
        for g in range(GROUPS)
    ).astype(jnp.bfloat16)
    for p in range(PARTS):
        out_ref[:, p * part_width : (p + 1) * part_width] = mixed[p * tokens : (p + 1) * tokens]


def body(tokens, expert_ids, gates, weights_in, weights_out):
    n = lax.axis_size("expert")
    flight = n // 2
    local, width = tokens.shape
    hid = weights_out.shape[1]
    part_width = width // PARTS
    dtype = tokens.dtype
    return pl.pallas_call(
        partial(kernel, n),
        out_shape=pltpu.VMEM((local, width), dtype),
        in_specs=[pl.BlockSpec(memory_space=pltpu.HBM)] * 5,
        out_specs=pl.BlockSpec(memory_space=pltpu.VMEM),
        scratch_shapes=[
            pltpu.VMEM((local, width), dtype),
            pltpu.VMEM(expert_ids.shape[::-1], expert_ids.dtype),
            pltpu.VMEM(gates.shape[::-1], gates.dtype),
            pltpu.VMEM(weights_in.shape[1:], weights_in.dtype),
            pltpu.VMEM(weights_out.shape[1:], weights_out.dtype),
            pltpu.VMEM((flight, GROUPS, PACK, part_width), dtype),
            pltpu.VMEM((n, GROUPS, PACK, part_width), dtype),
            pltpu.VMEM((n, GROUPS, PACK, part_width), dtype),
            pltpu.VMEM((n, GROUPS, PACK, part_width), dtype),
            pltpu.SemaphoreType.DMA((3,)),
            pltpu.SemaphoreType.DMA((2,)),
            pltpu.SemaphoreType.DMA,
            pltpu.SemaphoreType.DMA((n, GROUPS)),
            pltpu.SemaphoreType.DMA((n, GROUPS)),
            pltpu.SemaphoreType.DMA((n, GROUPS)),
            pltpu.SemaphoreType.DMA((n, GROUPS)),
            pltpu.SemaphoreType.DMA((n, GROUPS)),
        ],
        compiler_params=pltpu.CompilerParams(
            collective_id=0, has_side_effects=True, vmem_limit_bytes=56 * 2**20
        ),
    )(tokens, expert_ids.T, gates.T, weights_in, weights_out)


def solution(mesh):
    return jax.shard_map(
        body,
        mesh=mesh,
        in_specs=(
            P(("dp", "expert"), None),
            P(("dp", "expert"), None),
            P(("dp", "expert"), None),
            P("expert", None, None),
            P("expert", None, None),
        ),
        out_specs=P(("dp", "expert"), None),
        check_vma=False,
    )
```

```python
from functools import partial

import jax
import jax.numpy as jnp
from jax import lax
from jax.experimental import pallas as pl
from jax.experimental.pallas import tpu as pltpu
from jax.sharding import PartitionSpec as P

SRC_CAP = 8
PACK = 2 * SRC_CAP
IN_CHUNKS = 2
OUT_CHUNKS = 2
RELAY_IN = 1
MESH = pl.DeviceIdType.MESH


def slot_matrix(value, routed, position, rows, rows_per_expert):
    tokens = value[0].shape[1]
    row = lax.broadcasted_iota(jnp.int32, (rows, tokens), 0)
    slot = (row % SRC_CAP).astype(jnp.float32)
    expert = row // rows_per_expert
    table = jnp.zeros((rows, tokens), jnp.float32)
    for e in range(len(value)):
        hit = (expert == e) & (position[e] == slot) & (routed[e] > 0.0)
        table = jnp.where(hit, value[e], table)
    return table


def split_halves(table, axis):
    half = (lax.broadcasted_iota(jnp.int32, table.shape, axis) // SRC_CAP) % 2
    zero = jnp.zeros_like(table)
    return jnp.where(half == 0, table, zero), jnp.where(half == 1, table, zero)


def kernel(
    n,
    tok_hbm,
    ids_hbm,
    gate_hbm,
    win_hbm,
    wout_hbm,
    out_ref,
    tok,
    ids,
    gate,
    win,
    wout,
    send_rows,
    recv_rows,
    send_out,
    recv_out,
    small_sem,
    win_sem,
    wout_sem,
    row_send_sem,
    row_recv_sem,
    out_send_sem,
    out_recv_sem,
    relay_sem,
):
    me = lax.axis_index("expert")
    flight = n // 2
    width = tok.shape[1]
    hid = wout.shape[0]
    in_width = width // IN_CHUNKS
    in_half = in_width // 2
    out_width = width // OUT_CHUNKS
    out_half = out_width // 2

    pair = me // 2
    partner = me + 1 - 2 * (me % 2)

    def wrapped(index, count):
        return jnp.where(index >= count, index - count, index)

    peers = [wrapped(me + d, n) for d in range(1, n)]
    other_pairs = [wrapped(pair + k, flight) for k in range(1, flight)]
    others = [2 * other + member for other in other_pairs for member in range(2)]
    nears = [2 * other + jnp.where(me < 2 * other, 0, 1) for other in other_pairs]
    fars = [4 * other + 1 - near for other, near in zip(other_pairs, nears)]
    near_to = [(other < pair) == (me == 2 * pair) for other in other_pairs for _ in range(2)]

    small = [
        pltpu.make_async_copy(ids_hbm, ids, small_sem.at[0]),
        pltpu.make_async_copy(gate_hbm, gate, small_sem.at[1]),
        pltpu.make_async_copy(tok_hbm, tok, small_sem.at[2]),
    ]
    for copy in small:
        copy.start()

    barrier = pltpu.get_barrier_semaphore()
    for peer in peers:
        pl.semaphore_signal(barrier, inc=1, device_id={"expert": peer}, device_id_type=MESH)

    def win_copy(c):
        rows = pl.ds(c * in_width, in_width)
        return pltpu.make_async_copy(win_hbm.at[0, rows], win.at[rows], win_sem.at[c])

    wout_copy = pltpu.make_async_copy(wout_hbm.at[0], wout, wout_sem)
    for c in range(IN_CHUNKS):
        win_copy(c).start()
    wout_copy.start()

    small[0].wait()
    small[1].wait()
    chosen = ids[...]
    gates = gate[...].astype(jnp.float32)
    tokens = chosen.shape[1]
    weight, routed = [], []
    for e in range(flight):
        match = chosen == e
        weight.append(jnp.sum(jnp.where(match, gates, 0.0), axis=0, keepdims=True))
        routed.append(jnp.sum(jnp.where(match, 1.0, 0.0), axis=0, keepdims=True))
    row = lax.broadcasted_iota(jnp.int32, (PACK, tokens), 0)
    marks = jnp.zeros((PACK, tokens), jnp.float32)
    for e in range(flight):
        marks = jnp.where(row == e, routed[e], marks)
    before = lax.broadcasted_iota(jnp.int32, (tokens, tokens), 0) < lax.broadcasted_iota(
        jnp.int32, (tokens, tokens), 1
    )
    ahead = jnp.dot(
        marks.astype(jnp.bfloat16),
        before.astype(jnp.float32).astype(jnp.bfloat16),
        preferred_element_type=jnp.float32,
    )
    position = [ahead[e : e + 1] for e in range(flight)]
    pick = slot_matrix(routed, routed, position, flight * PACK, PACK)
    pick = [part.astype(jnp.bfloat16) for part in split_halves(pick, 0)]

    def row_copy(dst, c):
        return pltpu.make_async_remote_copy(
            src_ref=send_rows.at[dst // 2, c],
            dst_ref=recv_rows.at[me, c],
            send_sem=row_send_sem.at[dst, c],
            recv_sem=row_recv_sem.at[me, c],
            device_id={"expert": dst},
            device_id_type=MESH,
        )

    def relay_copy(src, c):
        return pltpu.make_async_remote_copy(
            src_ref=recv_rows.at[src, c],
            dst_ref=recv_rows.at[src, c],
            send_sem=relay_sem.at[src, c],
            recv_sem=row_recv_sem.at[src, c],
            device_id={"expert": partner},
            device_id_type=MESH,
        )

    def row_targets(c):
        return (fars if c >= RELAY_IN else []) + nears + [partner]

    small[2].wait()
    for c in range(IN_CHUNKS):
        lo = c * in_width
        rows = sum(
            jnp.dot(
                pick[half],
                tok[:, lo + half * in_half : lo + (half + 1) * in_half],
                preferred_element_type=jnp.float32,
            )
            for half in range(2)
        ).astype(jnp.bfloat16)
        send_rows[:, c] = rows.reshape(flight, PACK, in_half)
        if c == 0:
            pl.semaphore_wait(barrier, n - 1)
        for dst in row_targets(c):
            row_copy(dst, c).start()
        recv_rows[me, c] = send_rows[me // 2, c]

    combine = jnp.transpose(slot_matrix(weight, routed, position, n * PACK, 2 * PACK))
    combine = jnp.concatenate(split_halves(combine, 1), axis=0).astype(jnp.bfloat16)

    outer = (me % 2 == 0) == (2 * pair < flight)

    merged = jnp.zeros((n * SRC_CAP, 2 * hid), jnp.float32)
    for step in range(IN_CHUNKS):
        c = jnp.where(outer, IN_CHUNKS - 1 - step, step)
        for src, near in zip(others, near_to):
            relay_copy(src, c).wait_recv()

            @pl.when(near & (c < RELAY_IN))
            def _():
                relay_copy(src, c).start()

        relay_copy(partner, c).wait_recv()
        win_copy(c).wait()
        packed = recv_rows[:, c].astype(jnp.float32)
        for half in range(2):
            rows = packed[:, half * SRC_CAP : (half + 1) * SRC_CAP].reshape(n * SRC_CAP, in_half)
            start = pl.multiple_of(c * in_width + half * in_half, in_half)
            merged = merged + jnp.dot(
                rows.astype(jnp.bfloat16),
                win[pl.ds(start, in_half)],
                preferred_element_type=jnp.float32,
            )

    left = merged[:, :hid]
    hidden = (left / (1.0 + jnp.exp(-left)) * merged[:, hid:]).astype(jnp.bfloat16)

    def out_copy(dst, c, slot):
        return pltpu.make_async_remote_copy(
            src_ref=send_out.at[dst, c],
            dst_ref=recv_out.at[slot, c],
            send_sem=out_send_sem.at[dst, c],
            recv_sem=out_recv_sem.at[slot, c],
            device_id={"expert": dst},
            device_id_type=MESH,
        )

    wout_copy.wait()
    for c in range(OUT_CHUNKS):
        lo = c * out_width
        output = jnp.dot(
            hidden, wout[:, lo : lo + out_width], preferred_element_type=jnp.float32
        ).reshape(n, SRC_CAP, out_width)
        packed = jnp.concatenate([output[:, :, :out_half], output[:, :, out_half:]], axis=1)
        send_out[:, c] = packed.astype(jnp.bfloat16)
        for dst in others:
            out_copy(dst, c, me).start()
        out_copy(partner, c, me).start()
        recv_out[me, c] = send_out[me, c]

    for c in range(IN_CHUNKS):
        for dst in row_targets(c):
            row_copy(dst, c).wait_send()
        if c < RELAY_IN:
            for src, near in zip(others, near_to):

                @pl.when(near)
                def _():
                    relay_copy(src, c).wait_send()

    for c in range(OUT_CHUNKS):
        lo = c * out_width
        for peer in others + [partner]:
            out_copy(peer, c, me).wait_send()
        for peer in others + [partner]:
            out_copy(partner, c, peer).wait_recv()
        packed = recv_out[:, c].reshape(n * PACK, out_half)
        mixed = jnp.dot(combine, packed, preferred_element_type=jnp.float32).astype(jnp.bfloat16)
        out_ref[:, lo : lo + out_half] = mixed[:tokens]
        out_ref[:, lo + out_half : lo + out_width] = mixed[tokens:]


def body(tokens, expert_ids, gates, weights_in, weights_out):
    n = lax.axis_size("expert")
    flight = n // 2
    local, width = tokens.shape
    hid = weights_out.shape[1]
    in_half = width // IN_CHUNKS // 2
    out_half = width // OUT_CHUNKS // 2
    dtype = tokens.dtype
    return pl.pallas_call(
        partial(kernel, n),
        out_shape=pltpu.VMEM((local, width), dtype),
        in_specs=[pl.BlockSpec(memory_space=pltpu.HBM)] * 5,
        out_specs=pl.BlockSpec(memory_space=pltpu.VMEM),
        scratch_shapes=[
            pltpu.VMEM((local, width), dtype),
            pltpu.VMEM(expert_ids.shape[::-1], expert_ids.dtype),
            pltpu.VMEM(gates.shape[::-1], gates.dtype),
            pltpu.VMEM(weights_in.shape[1:], weights_in.dtype),
            pltpu.VMEM(weights_out.shape[1:], weights_out.dtype),
            pltpu.VMEM((flight, IN_CHUNKS, PACK, in_half), dtype),
            pltpu.VMEM((n, IN_CHUNKS, PACK, in_half), dtype),
            pltpu.VMEM((n, OUT_CHUNKS, PACK, out_half), dtype),
            pltpu.VMEM((n, OUT_CHUNKS, PACK, out_half), dtype),
            pltpu.SemaphoreType.DMA((3,)),
            pltpu.SemaphoreType.DMA((IN_CHUNKS,)),
            pltpu.SemaphoreType.DMA,
            pltpu.SemaphoreType.DMA((n, IN_CHUNKS)),
            pltpu.SemaphoreType.DMA((n, IN_CHUNKS)),
            pltpu.SemaphoreType.DMA((n, OUT_CHUNKS)),
            pltpu.SemaphoreType.DMA((n, OUT_CHUNKS)),
            pltpu.SemaphoreType.DMA((n, IN_CHUNKS)),
        ],
        compiler_params=pltpu.CompilerParams(
            collective_id=0, has_side_effects=True, vmem_limit_bytes=56 * 2**20
        ),
    )(tokens, expert_ids.T, gates.T, weights_in, weights_out)


def solution(mesh):
    return jax.shard_map(
        body,
        mesh=mesh,
        in_specs=(
            P(("dp", "expert"), None),
            P(("dp", "expert"), None),
            P(("dp", "expert"), None),
            P("expert", None, None),
            P("expert", None, None),
        ),
        out_specs=P(("dp", "expert"), None),
        check_vma=False,
    )
```

```python
from functools import partial

import jax
import jax.numpy as jnp
from jax import lax
from jax.experimental import pallas as pl
from jax.experimental.pallas import tpu as pltpu
from jax.sharding import PartitionSpec as P

SRC_CAP = 8
PACK = 2 * SRC_CAP
IN_CHUNKS = 4
OUT_CHUNKS = 2
RELAY_IN = 2
MESH = pl.DeviceIdType.MESH


def slot_matrix(value, routed, position, rows, rows_per_expert):
    tokens = value[0].shape[1]
    row = lax.broadcasted_iota(jnp.int32, (rows, tokens), 0)
    slot = (row % SRC_CAP).astype(jnp.float32)
    expert = row // rows_per_expert
    table = jnp.zeros((rows, tokens), jnp.float32)
    for e in range(len(value)):
        hit = (expert == e) & (position[e] == slot) & (routed[e] > 0.0)
        table = jnp.where(hit, value[e], table)
    return table


def split_halves(table, axis):
    half = (lax.broadcasted_iota(jnp.int32, table.shape, axis) // SRC_CAP) % 2
    zero = jnp.zeros_like(table)
    return jnp.where(half == 0, table, zero), jnp.where(half == 1, table, zero)


def kernel(
    n,
    tok_hbm,
    ids_hbm,
    gate_hbm,
    win_hbm,
    wout_hbm,
    out_ref,
    tok,
    ids,
    gate,
    win,
    wout,
    send_rows,
    recv_rows,
    send_out,
    recv_out,
    small_sem,
    win_sem,
    wout_sem,
    row_send_sem,
    row_recv_sem,
    out_send_sem,
    out_recv_sem,
    relay_sem,
):
    me = lax.axis_index("expert")
    flight = n // 2
    width = tok.shape[1]
    hid = wout.shape[0]
    in_width = width // IN_CHUNKS
    in_half = in_width // 2
    out_width = width // OUT_CHUNKS
    out_half = out_width // 2

    pair = me // 2
    partner = me + 1 - 2 * (me % 2)

    def wrapped(index, count):
        return jnp.where(index >= count, index - count, index)

    peers = [wrapped(me + d, n) for d in range(1, n)]
    other_pairs = [wrapped(pair + k, flight) for k in range(1, flight)]
    others = [2 * other + member for other in other_pairs for member in range(2)]
    nears = [2 * other + jnp.where(me < 2 * other, 0, 1) for other in other_pairs]
    fars = [4 * other + 1 - near for other, near in zip(other_pairs, nears)]
    near_to = [(other < pair) == (me == 2 * pair) for other in other_pairs for _ in range(2)]

    small = [
        pltpu.make_async_copy(ids_hbm, ids, small_sem.at[0]),
        pltpu.make_async_copy(gate_hbm, gate, small_sem.at[1]),
        pltpu.make_async_copy(tok_hbm, tok, small_sem.at[2]),
    ]
    for copy in small:
        copy.start()

    barrier = pltpu.get_barrier_semaphore()
    for peer in peers:
        pl.semaphore_signal(barrier, inc=1, device_id={"expert": peer}, device_id_type=MESH)

    def win_copy(c):
        rows = pl.ds(c * in_width, in_width)
        return pltpu.make_async_copy(win_hbm.at[0, rows], win.at[rows], win_sem.at[c])

    wout_copy = pltpu.make_async_copy(wout_hbm.at[0], wout, wout_sem)
    for c in range(IN_CHUNKS):
        win_copy(c).start()
    wout_copy.start()

    small[0].wait()
    small[1].wait()
    chosen = ids[...]
    gates = gate[...].astype(jnp.float32)
    tokens = chosen.shape[1]
    weight, routed = [], []
    for e in range(flight):
        match = chosen == e
        weight.append(jnp.sum(jnp.where(match, gates, 0.0), axis=0, keepdims=True))
        routed.append(jnp.sum(jnp.where(match, 1.0, 0.0), axis=0, keepdims=True))
    row = lax.broadcasted_iota(jnp.int32, (PACK, tokens), 0)
    marks = jnp.zeros((PACK, tokens), jnp.float32)
    for e in range(flight):
        marks = jnp.where(row == e, routed[e], marks)
    before = lax.broadcasted_iota(jnp.int32, (tokens, tokens), 0) < lax.broadcasted_iota(
        jnp.int32, (tokens, tokens), 1
    )
    ahead = jnp.dot(
        marks.astype(jnp.bfloat16),
        before.astype(jnp.float32).astype(jnp.bfloat16),
        preferred_element_type=jnp.float32,
    )
    position = [ahead[e : e + 1] for e in range(flight)]
    pick = slot_matrix(routed, routed, position, flight * PACK, PACK)
    pick = [part.astype(jnp.bfloat16) for part in split_halves(pick, 0)]

    def row_copy(dst, c):
        return pltpu.make_async_remote_copy(
            src_ref=send_rows.at[dst // 2, c],
            dst_ref=recv_rows.at[me, c],
            send_sem=row_send_sem.at[dst, c],
            recv_sem=row_recv_sem.at[me, c],
            device_id={"expert": dst},
            device_id_type=MESH,
        )

    def relay_copy(src, c):
        return pltpu.make_async_remote_copy(
            src_ref=recv_rows.at[src, c],
            dst_ref=recv_rows.at[src, c],
            send_sem=relay_sem.at[src, c],
            recv_sem=row_recv_sem.at[src, c],
            device_id={"expert": partner},
            device_id_type=MESH,
        )

    def row_targets(c):
        return (fars if c >= RELAY_IN else []) + nears + [partner]

    small[2].wait()
    for c in range(IN_CHUNKS):
        lo = c * in_width
        rows = sum(
            jnp.dot(
                pick[half],
                tok[:, lo + half * in_half : lo + (half + 1) * in_half],
                preferred_element_type=jnp.float32,
            )
            for half in range(2)
        ).astype(jnp.bfloat16)
        send_rows[:, c] = rows.reshape(flight, PACK, in_half)
        if c == 0:
            pl.semaphore_wait(barrier, n - 1)
        for dst in row_targets(c):
            row_copy(dst, c).start()
        recv_rows[me, c] = send_rows[me // 2, c]

    combine = jnp.transpose(slot_matrix(weight, routed, position, n * PACK, 2 * PACK))
    combine = jnp.concatenate(split_halves(combine, 1), axis=0).astype(jnp.bfloat16)

    outer = (me % 2 == 0) == (2 * pair < flight)

    merged = jnp.zeros((n * SRC_CAP, 2 * hid), jnp.float32)
    for step in range(IN_CHUNKS):
        c = jnp.where(outer, (step + RELAY_IN) % IN_CHUNKS, step)
        for src, near in zip(others, near_to):
            relay_copy(src, c).wait_recv()

            @pl.when(near & (c < RELAY_IN))
            def _():
                relay_copy(src, c).start()

        relay_copy(partner, c).wait_recv()
        win_copy(c).wait()
        packed = recv_rows[:, c].astype(jnp.float32)
        for half in range(2):
            rows = packed[:, half * SRC_CAP : (half + 1) * SRC_CAP].reshape(n * SRC_CAP, in_half)
            start = pl.multiple_of(c * in_width + half * in_half, in_half)
            merged = merged + jnp.dot(
                rows.astype(jnp.bfloat16),
                win[pl.ds(start, in_half)],
                preferred_element_type=jnp.float32,
            )

    left = merged[:, :hid]
    hidden = (left / (1.0 + jnp.exp(-left)) * merged[:, hid:]).astype(jnp.bfloat16)

    def out_copy(dst, c, slot):
        return pltpu.make_async_remote_copy(
            src_ref=send_out.at[dst, c],
            dst_ref=recv_out.at[slot, c],
            send_sem=out_send_sem.at[dst, c],
            recv_sem=out_recv_sem.at[slot, c],
            device_id={"expert": dst},
            device_id_type=MESH,
        )

    wout_copy.wait()
    for c in range(OUT_CHUNKS):
        lo = c * out_width
        output = jnp.dot(
            hidden, wout[:, lo : lo + out_width], preferred_element_type=jnp.float32
        ).reshape(n, SRC_CAP, out_width)
        packed = jnp.concatenate([output[:, :, :out_half], output[:, :, out_half:]], axis=1)
        send_out[:, c] = packed.astype(jnp.bfloat16)
        for dst in others:
            out_copy(dst, c, me).start()
        out_copy(partner, c, me).start()
        recv_out[me, c] = send_out[me, c]

    for c in range(IN_CHUNKS):
        for dst in row_targets(c):
            row_copy(dst, c).wait_send()
        if c < RELAY_IN:
            for src, near in zip(others, near_to):

                @pl.when(near)
                def _():
                    relay_copy(src, c).wait_send()

    for c in range(OUT_CHUNKS):
        lo = c * out_width
        for peer in others + [partner]:
            out_copy(peer, c, me).wait_send()
        for peer in others + [partner]:
            out_copy(partner, c, peer).wait_recv()
        packed = recv_out[:, c].reshape(n * PACK, out_half)
        mixed = jnp.dot(combine, packed, preferred_element_type=jnp.float32).astype(jnp.bfloat16)
        out_ref[:, lo : lo + out_half] = mixed[:tokens]
        out_ref[:, lo + out_half : lo + out_width] = mixed[tokens:]


def body(tokens, expert_ids, gates, weights_in, weights_out):
    n = lax.axis_size("expert")
    flight = n // 2
    local, width = tokens.shape
    hid = weights_out.shape[1]
    in_half = width // IN_CHUNKS // 2
    out_half = width // OUT_CHUNKS // 2
    dtype = tokens.dtype
    return pl.pallas_call(
        partial(kernel, n),
        out_shape=pltpu.VMEM((local, width), dtype),
        in_specs=[pl.BlockSpec(memory_space=pltpu.HBM)] * 5,
        out_specs=pl.BlockSpec(memory_space=pltpu.VMEM),
        scratch_shapes=[
            pltpu.VMEM((local, width), dtype),
            pltpu.VMEM(expert_ids.shape[::-1], expert_ids.dtype),
            pltpu.VMEM(gates.shape[::-1], gates.dtype),
            pltpu.VMEM(weights_in.shape[1:], weights_in.dtype),
            pltpu.VMEM(weights_out.shape[1:], weights_out.dtype),
            pltpu.VMEM((flight, IN_CHUNKS, PACK, in_half), dtype),
            pltpu.VMEM((n, IN_CHUNKS, PACK, in_half), dtype),
            pltpu.VMEM((n, OUT_CHUNKS, PACK, out_half), dtype),
            pltpu.VMEM((n, OUT_CHUNKS, PACK, out_half), dtype),
            pltpu.SemaphoreType.DMA((3,)),
            pltpu.SemaphoreType.DMA((IN_CHUNKS,)),
            pltpu.SemaphoreType.DMA,
            pltpu.SemaphoreType.DMA((n, IN_CHUNKS)),
            pltpu.SemaphoreType.DMA((n, IN_CHUNKS)),
            pltpu.SemaphoreType.DMA((n, OUT_CHUNKS)),
            pltpu.SemaphoreType.DMA((n, OUT_CHUNKS)),
            pltpu.SemaphoreType.DMA((n, IN_CHUNKS)),
        ],
        compiler_params=pltpu.CompilerParams(
            collective_id=0, has_side_effects=True, vmem_limit_bytes=56 * 2**20
        ),
    )(tokens, expert_ids.T, gates.T, weights_in, weights_out)


def solution(mesh):
    return jax.shard_map(
        body,
        mesh=mesh,
        in_specs=(
            P(("dp", "expert"), None),
            P(("dp", "expert"), None),
            P(("dp", "expert"), None),
            P("expert", None, None),
            P("expert", None, None),
        ),
        out_specs=P(("dp", "expert"), None),
        check_vma=False,
    )
```

```python
from functools import partial

import jax
import jax.numpy as jnp
from jax import lax
from jax.experimental import pallas as pl
from jax.experimental.pallas import tpu as pltpu
from jax.sharding import PartitionSpec as P

SRC_CAP = 8
PACK = 2 * SRC_CAP
IN_CHUNKS = 4
OUT_CHUNKS = 2
RELAY_IN = 3
MESH = pl.DeviceIdType.MESH


def slot_matrix(value, routed, position, rows, rows_per_expert):
    tokens = value[0].shape[1]
    row = lax.broadcasted_iota(jnp.int32, (rows, tokens), 0)
    slot = (row % SRC_CAP).astype(jnp.float32)
    expert = row // rows_per_expert
    table = jnp.zeros((rows, tokens), jnp.float32)
    for e in range(len(value)):
        hit = (expert == e) & (position[e] == slot) & (routed[e] > 0.0)
        table = jnp.where(hit, value[e], table)
    return table


def split_halves(table, axis):
    half = (lax.broadcasted_iota(jnp.int32, table.shape, axis) // SRC_CAP) % 2
    zero = jnp.zeros_like(table)
    return jnp.where(half == 0, table, zero), jnp.where(half == 1, table, zero)


def kernel(
    n,
    tok_hbm,
    ids_hbm,
    gate_hbm,
    win_hbm,
    wout_hbm,
    out_ref,
    tok,
    ids,
    gate,
    win,
    wout,
    send_rows,
    recv_rows,
    send_out,
    recv_out,
    small_sem,
    win_sem,
    wout_sem,
    row_send_sem,
    row_recv_sem,
    out_send_sem,
    out_recv_sem,
    relay_sem,
):
    me = lax.axis_index("expert")
    flight = n // 2
    width = tok.shape[1]
    hid = wout.shape[0]
    in_width = width // IN_CHUNKS
    in_half = in_width // 2
    out_width = width // OUT_CHUNKS
    out_half = out_width // 2

    pair = me // 2
    partner = me + 1 - 2 * (me % 2)

    def wrapped(index, count):
        return jnp.where(index >= count, index - count, index)

    peers = [wrapped(me + d, n) for d in range(1, n)]
    other_pairs = [wrapped(pair + k, flight) for k in range(1, flight)]
    others = [2 * other + member for other in other_pairs for member in range(2)]
    nears = [2 * other + jnp.where(me < 2 * other, 0, 1) for other in other_pairs]
    fars = [4 * other + 1 - near for other, near in zip(other_pairs, nears)]
    near_to = [(other < pair) == (me == 2 * pair) for other in other_pairs for _ in range(2)]

    small = [
        pltpu.make_async_copy(ids_hbm, ids, small_sem.at[0]),
        pltpu.make_async_copy(gate_hbm, gate, small_sem.at[1]),
        pltpu.make_async_copy(tok_hbm, tok, small_sem.at[2]),
    ]
    for copy in small:
        copy.start()

    barrier = pltpu.get_barrier_semaphore()
    for peer in peers:
        pl.semaphore_signal(barrier, inc=1, device_id={"expert": peer}, device_id_type=MESH)

    def win_copy(c):
        rows = pl.ds(c * in_width, in_width)
        return pltpu.make_async_copy(win_hbm.at[0, rows], win.at[rows], win_sem.at[c])

    wout_copy = pltpu.make_async_copy(wout_hbm.at[0], wout, wout_sem)
    for c in range(IN_CHUNKS):
        win_copy(c).start()
    wout_copy.start()

    small[0].wait()
    small[1].wait()
    chosen = ids[...]
    gates = gate[...].astype(jnp.float32)
    tokens = chosen.shape[1]
    weight, routed = [], []
    for e in range(flight):
        match = chosen == e
        weight.append(jnp.sum(jnp.where(match, gates, 0.0), axis=0, keepdims=True))
        routed.append(jnp.sum(jnp.where(match, 1.0, 0.0), axis=0, keepdims=True))
    row = lax.broadcasted_iota(jnp.int32, (PACK, tokens), 0)
    marks = jnp.zeros((PACK, tokens), jnp.float32)
    for e in range(flight):
        marks = jnp.where(row == e, routed[e], marks)
    before = lax.broadcasted_iota(jnp.int32, (tokens, tokens), 0) < lax.broadcasted_iota(
        jnp.int32, (tokens, tokens), 1
    )
    ahead = jnp.dot(
        marks.astype(jnp.bfloat16),
        before.astype(jnp.float32).astype(jnp.bfloat16),
        preferred_element_type=jnp.float32,
    )
    position = [ahead[e : e + 1] for e in range(flight)]
    pick = slot_matrix(routed, routed, position, flight * PACK, PACK)
    pick = [part.astype(jnp.bfloat16) for part in split_halves(pick, 0)]

    def row_copy(dst, c):
        return pltpu.make_async_remote_copy(
            src_ref=send_rows.at[dst // 2, c],
            dst_ref=recv_rows.at[me, c],
            send_sem=row_send_sem.at[dst, c],
            recv_sem=row_recv_sem.at[me, c],
            device_id={"expert": dst},
            device_id_type=MESH,
        )

    def relay_copy(src, c):
        return pltpu.make_async_remote_copy(
            src_ref=recv_rows.at[src, c],
            dst_ref=recv_rows.at[src, c],
            send_sem=relay_sem.at[src, c],
            recv_sem=row_recv_sem.at[src, c],
            device_id={"expert": partner},
            device_id_type=MESH,
        )

    def row_targets(c):
        return (fars if c >= RELAY_IN else []) + nears + [partner]

    small[2].wait()
    for c in range(IN_CHUNKS):
        lo = c * in_width
        rows = sum(
            jnp.dot(
                pick[half],
                tok[:, lo + half * in_half : lo + (half + 1) * in_half],
                preferred_element_type=jnp.float32,
            )
            for half in range(2)
        ).astype(jnp.bfloat16)
        send_rows[:, c] = rows.reshape(flight, PACK, in_half)
        if c == 0:
            pl.semaphore_wait(barrier, n - 1)
        for dst in row_targets(c):
            row_copy(dst, c).start()
        recv_rows[me, c] = send_rows[me // 2, c]

    combine = jnp.transpose(slot_matrix(weight, routed, position, n * PACK, 2 * PACK))
    combine = jnp.concatenate(split_halves(combine, 1), axis=0).astype(jnp.bfloat16)

    outer = (me % 2 == 0) == (2 * pair < flight)

    merged = jnp.zeros((n * SRC_CAP, 2 * hid), jnp.float32)
    for step in range(IN_CHUNKS):
        c = jnp.where(outer, (step + RELAY_IN) % IN_CHUNKS, step)
        for src, near in zip(others, near_to):
            relay_copy(src, c).wait_recv()

            @pl.when(near & (c < RELAY_IN))
            def _():
                relay_copy(src, c).start()

        relay_copy(partner, c).wait_recv()
        win_copy(c).wait()
        packed = recv_rows[:, c].astype(jnp.float32)
        for half in range(2):
            rows = packed[:, half * SRC_CAP : (half + 1) * SRC_CAP].reshape(n * SRC_CAP, in_half)
            start = pl.multiple_of(c * in_width + half * in_half, in_half)
            merged = merged + jnp.dot(
                rows.astype(jnp.bfloat16),
                win[pl.ds(start, in_half)],
                preferred_element_type=jnp.float32,
            )

    left = merged[:, :hid]
    hidden = (left / (1.0 + jnp.exp(-left)) * merged[:, hid:]).astype(jnp.bfloat16)

    def out_copy(dst, c, slot):
        return pltpu.make_async_remote_copy(
            src_ref=send_out.at[dst, c],
            dst_ref=recv_out.at[slot, c],
            send_sem=out_send_sem.at[dst, c],
            recv_sem=out_recv_sem.at[slot, c],
            device_id={"expert": dst},
            device_id_type=MESH,
        )

    wout_copy.wait()
    for c in range(OUT_CHUNKS):
        lo = c * out_width
        output = jnp.dot(
            hidden, wout[:, lo : lo + out_width], preferred_element_type=jnp.float32
        ).reshape(n, SRC_CAP, out_width)
        packed = jnp.concatenate([output[:, :, :out_half], output[:, :, out_half:]], axis=1)
        send_out[:, c] = packed.astype(jnp.bfloat16)
        for dst in others:
            out_copy(dst, c, me).start()
        out_copy(partner, c, me).start()
        recv_out[me, c] = send_out[me, c]

    for c in range(IN_CHUNKS):
        for dst in row_targets(c):
            row_copy(dst, c).wait_send()
        if c < RELAY_IN:
            for src, near in zip(others, near_to):

                @pl.when(near)
                def _():
                    relay_copy(src, c).wait_send()

    for c in range(OUT_CHUNKS):
        lo = c * out_width
        for peer in others + [partner]:
            out_copy(peer, c, me).wait_send()
        for peer in others + [partner]:
            out_copy(partner, c, peer).wait_recv()
        packed = recv_out[:, c].reshape(n * PACK, out_half)
        mixed = jnp.dot(combine, packed, preferred_element_type=jnp.float32).astype(jnp.bfloat16)
        out_ref[:, lo : lo + out_half] = mixed[:tokens]
        out_ref[:, lo + out_half : lo + out_width] = mixed[tokens:]


def body(tokens, expert_ids, gates, weights_in, weights_out):
    n = lax.axis_size("expert")
    flight = n // 2
    local, width = tokens.shape
    hid = weights_out.shape[1]
    in_half = width // IN_CHUNKS // 2
    out_half = width // OUT_CHUNKS // 2
    dtype = tokens.dtype
    return pl.pallas_call(
        partial(kernel, n),
        out_shape=pltpu.VMEM((local, width), dtype),
        in_specs=[pl.BlockSpec(memory_space=pltpu.HBM)] * 5,
        out_specs=pl.BlockSpec(memory_space=pltpu.VMEM),
        scratch_shapes=[
            pltpu.VMEM((local, width), dtype),
            pltpu.VMEM(expert_ids.shape[::-1], expert_ids.dtype),
            pltpu.VMEM(gates.shape[::-1], gates.dtype),
            pltpu.VMEM(weights_in.shape[1:], weights_in.dtype),
            pltpu.VMEM(weights_out.shape[1:], weights_out.dtype),
            pltpu.VMEM((flight, IN_CHUNKS, PACK, in_half), dtype),
            pltpu.VMEM((n, IN_CHUNKS, PACK, in_half), dtype),
            pltpu.VMEM((n, OUT_CHUNKS, PACK, out_half), dtype),
            pltpu.VMEM((n, OUT_CHUNKS, PACK, out_half), dtype),
            pltpu.SemaphoreType.DMA((3,)),
            pltpu.SemaphoreType.DMA((IN_CHUNKS,)),
            pltpu.SemaphoreType.DMA,
            pltpu.SemaphoreType.DMA((n, IN_CHUNKS)),
            pltpu.SemaphoreType.DMA((n, IN_CHUNKS)),
            pltpu.SemaphoreType.DMA((n, OUT_CHUNKS)),
            pltpu.SemaphoreType.DMA((n, OUT_CHUNKS)),
            pltpu.SemaphoreType.DMA((n, IN_CHUNKS)),
        ],
        compiler_params=pltpu.CompilerParams(
            collective_id=0, has_side_effects=True, vmem_limit_bytes=56 * 2**20
        ),
    )(tokens, expert_ids.T, gates.T, weights_in, weights_out)


def solution(mesh):
    return jax.shard_map(
        body,
        mesh=mesh,
        in_specs=(
            P(("dp", "expert"), None),
            P(("dp", "expert"), None),
            P(("dp", "expert"), None),
            P("expert", None, None),
            P("expert", None, None),
        ),
        out_specs=P(("dp", "expert"), None),
        check_vma=False,
    )
```
